32 devices in a mesh: batch: 16 (over z, y, x), seq: 2 (over core).
Axes of the slice: x: 2, y: 2, z: 4, core: 2. Of those that a mesh axis runs over, the one named last changes fastest.
Arguments:
- tokens: bfloat16 [32768, 768], P(('batch', 'seq')), may hold values from -6 to 6
- seq_lengths: int32 [16, 3], P('batch'), may hold values from 256 to 1024, as said below
- first_gain: float32 [768], replicated, may hold values from 0.5 to 1.5
- first_shift: float32 [768], replicated, may hold values from -2 to 2
- qkv_weight: bfloat16 [768, 2304], replicated, may hold values from -0.21875 to 0.21875
- query_bias: float32 [768], replicated, may hold values from -2 to 2
- value_bias: float32 [768], replicated, may hold values from -2 to 2
- proj_weight: bfloat16 [768, 768], replicated, may hold values from -3.5 to 3.5
- proj_bias: float32 [768], replicated, may hold values from -2 to 2
- second_gain: float32 [768], replicated, may hold values from 0.5 to 1.5
- second_shift: float32 [768], replicated, may hold values from -2 to 2
- expand_weight: bfloat16 [768, 3072], replicated, may hold values from -0.21875 to 0.21875
- expand_bias: float32 [3072], replicated, may hold values from -2 to 2
- shrink_weight: bfloat16 [3072, 768], replicated, may hold values from -0.109375 to 0.109375
- shrink_bias: float32 [768], replicated, may hold values from -2 to 2
- cotangent: bfloat16 [32768, 768], P(('batch', 'seq')), may hold values from -6 to 6
Outputs:
- output: bfloat16 [32768, 768], P(('batch', 'seq'))
- input_grad: float32 [32768, 768], P(('batch', 'seq'))
- grad_first_gain: float32 [768], P(('batch', 'seq'))
- grad_first_shift: float32 [768], P(('batch', 'seq'))
- grad_qkv_weight: float32 [768, 2304], P(('batch', 'seq'))
- grad_query_bias: float32 [768], P(('batch', 'seq'))
- grad_value_bias: float32 [768], P(('batch', 'seq'))
- grad_proj_weight: float32 [768, 768], P(('batch', 'seq'))
- grad_proj_bias: float32 [768], P(('batch', 'seq'))
- grad_second_gain: float32 [768], P(('batch', 'seq'))
- grad_second_shift: float32 [768], P(('batch', 'seq'))
- grad_expand_weight: float32 [768, 3072], P(('batch', 'seq'))
- grad_expand_bias: float32 [3072], P(('batch', 'seq'))
- grad_shrink_weight: float32 [3072, 768], P(('batch', 'seq'))
- grad_shrink_bias: float32 [768], P(('batch', 'seq'))
The draws below stay inside these ranges and needn't reach their ends.
Inputs may be any that keep to these rules, and one draw needn't show every extreme that they name: `seq_lengths`: row g lists the lengths of the three sequences packed in order into group g; they sum to 2048 and the middle one has exactly 1024 tokens.
All inputs are finite; a program needn't handle non-finite values.
Results may differ from the reference program's by a relative error of at most 0.01.
Values may be sent and summed in bfloat16 or wider, within the bound.
A program may use at most 320 MiB of HBM per device.

```python
import math
import jax
import jax.numpy as jnp
from jax import lax

D = 768
H = 12
HD = 64
FF = 3072
TOK_DEV = 1024
GROUP = 2048
LONG = 1024
GROUPS = 16
TOKENS = 32768


def draw_seq_lengths(key, part):
    key = jax.random.fold_in(key, 11)
    first_length = jax.random.randint(key, (GROUPS,), TOK_DEV // 4, 3 * TOK_DEV // 4 + 1)
    middle_length = jnp.zeros((GROUPS,), jnp.int32) + LONG
    last_length = GROUP - LONG - first_length
    return jnp.stack([first_length, middle_length, last_length], axis=1).astype(jnp.int32)


def levels(rng, shape, cuts, low, high):
    loudness = 1.0
    for dim, parts in cuts:
        steps = jax.random.uniform(jax.random.fold_in(jax.random.fold_in(rng, 6), dim), (parts,), jnp.float32, low / len(cuts), high / len(cuts))
        loudness = loudness * jnp.repeat(jnp.exp(steps), shape[dim] // parts).reshape((-1,) + (1,) * (len(shape) - 1 - dim))
    return loudness


def bell_draw(stream_key, shape, spread, limit, cuts=(), kind=jnp.bfloat16):
    drawn = jax.random.normal(stream_key, shape, jnp.float32) * spread
    if len(cuts) > 0:
        drawn = levels(stream_key, shape, cuts, -0.22, 0.18) * drawn
    return jnp.clip(drawn, min=-limit, max=limit).astype(kind)


def setup_inputs(seed: int = 0) -> dict:
    key_of = jax.random.split(jax.random.key(seed), 17)
    tokens = bell_draw(key_of[0], (TOKENS, D), 1.0, 6.0, ((0, 32),))
    seq_lengths = draw_seq_lengths(jax.random.fold_in(key_of[16], 71), 0)
    first_gain = jnp.clip(1.0 + 0.1 * jax.random.normal(key_of[2], (D,), jnp.float32), 0.5, 1.5)
    first_shift = bell_draw(key_of[3], (D,), 0.3, 2.0, (), jnp.float32)
    qkv_weight = bell_draw(key_of[4], (D, 3 * D), D ** -0.5, 0.21875)
    query_bias = bell_draw(key_of[5], (D,), 0.3, 2.0, (), jnp.float32)
    value_bias = bell_draw(key_of[6], (D,), 0.3, 2.0, (), jnp.float32)
    proj_weight = bell_draw(key_of[7], (D, D), (max(1, D // 256)) ** -0.5, 3.5)
    proj_bias = bell_draw(key_of[8], (D,), 0.3, 2.0, (), jnp.float32)
    second_gain = jnp.clip(1.0 + 0.1 * jax.random.normal(key_of[9], (D,), jnp.float32), 0.5, 1.5)
    second_shift = bell_draw(key_of[10], (D,), 0.3, 2.0, (), jnp.float32)
    expand_weight = bell_draw(key_of[11], (D, FF), D ** -0.5, 0.21875)
    expand_bias = bell_draw(key_of[12], (FF,), 0.3, 2.0, (), jnp.float32)
    shrink_weight = bell_draw(key_of[13], (FF, D), FF ** -0.5, 0.109375)
    shrink_bias = bell_draw(key_of[14], (D,), 0.3, 2.0, (), jnp.float32)
    cotangent = bell_draw(key_of[15], (TOKENS, D), 1.0, 6.0, ((0, 32),))
    return {"tokens": tokens, "seq_lengths": seq_lengths, "first_gain": first_gain, "first_shift": first_shift, "qkv_weight": qkv_weight, "query_bias": query_bias, "value_bias": value_bias, "proj_weight": proj_weight, "proj_bias": proj_bias, "second_gain": second_gain, "second_shift": second_shift, "expand_weight": expand_weight, "expand_bias": expand_bias, "shrink_weight": shrink_weight, "shrink_bias": shrink_bias, "cotangent": cotangent}


epsilon = 1e-05
highest_mode = lax.Precision.HIGHEST

@jax.custom_vjp
def low(v):
    return lax.optimization_barrier(v.astype(jnp.bfloat16)).astype(jnp.float32)

@jax.custom_vjp
def low_back(v):
    return v

def low_keep(v):
    return (low(v), None)

def low_pass(kept, grad):
    return (grad,)

def back_keep(v):
    return (v, None)

def back_low(kept, grad):
    return (low(grad),)
low.defvjp(low_keep, low_pass)
low_back.defvjp(back_keep, back_low)

def layer_norm(v, norm_gain, norm_shift):
    row_mean = lax.optimization_barrier(jnp.mean(v, axis=-1, keepdims=True))
    centered = v - row_mean
    row_var = lax.optimization_barrier(jnp.mean(centered * centered, axis=-1, keepdims=True))
    return centered * lax.rsqrt(row_var + epsilon) * norm_gain + norm_shift

def gelu_tanh(v):
    return 0.5 * v * (1.0 + jnp.tanh(0.7978845608028654 * (v + 0.044715 * v * v * v)))

def highest(a, b):
    return jnp.dot(a, b, precision=highest_mode, preferred_element_type=jnp.float32)

def to_heads(t):
    return jnp.transpose(t, (1, 0, 2))

def group_attention(pieces):
    query_group, key_group, value_group, lengths = pieces
    group_rows = query_group.shape[0]
    places = jnp.arange(group_rows, dtype=jnp.int32)
    segment = (places >= lengths[0]).astype(jnp.int32) + (places >= lengths[0] + lengths[1]).astype(jnp.int32)
    allowed = (places[None, :] <= places[:, None]) & (segment[None, :] == segment[:, None])
    score_scale = 1.0 / math.sqrt(HD)

    def head_attention(head_parts):
        query_head, key_head, value_head = head_parts
        scores = low_back(highest(query_head, key_head.T) * score_scale)
        scores = jnp.where(allowed, scores, -1e+30)
        row_peak = lax.optimization_barrier(jnp.max(scores, axis=-1, keepdims=True))
        weights = jnp.exp(scores - row_peak)
        softmax_rows = weights / lax.optimization_barrier(jnp.sum(weights, axis=-1, keepdims=True))
        return highest(low(softmax_rows), value_head)
    context = lax.map(head_attention, (to_heads(query_group), to_heads(key_group), to_heads(value_group)))
    return to_heads(context)

def layer_forward(tokens, first_gain, first_shift, qkv_weight, query_bias, value_bias, proj_weight, proj_bias, second_gain, second_shift, expand_weight, expand_bias, shrink_weight, shrink_bias, seq_lengths):
    total_rows = tokens.shape[0]
    normed_first = low(layer_norm(tokens, first_gain, first_shift))
    projected = highest(normed_first, qkv_weight)
    queries = low_back(low(projected[:, :D] + query_bias))
    key_rows = low_back(low(projected[:, D:2 * D]))
    values = low_back(low(projected[:, 2 * D:] + value_bias))
    group_count = total_rows // GROUP

    def by_group(t):
        return t.reshape(group_count, GROUP, H, HD)
    context = lax.map(jax.checkpoint(group_attention), (by_group(queries), by_group(key_rows), by_group(values), seq_lengths))
    context = low_back(low(context.reshape(total_rows, D)))
    attended = low_back(highest(context, proj_weight) + proj_bias)
    middle = tokens + attended
    normed_second = low(layer_norm(middle, second_gain, second_shift))
    expanded = low_back(highest(normed_second, expand_weight) + expand_bias)
    activated = low(gelu_tanh(expanded))
    shrunk = low_back(highest(activated, shrink_weight) + shrink_bias)
    return middle + shrunk

def reference(tokens, seq_lengths, first_gain, first_shift, qkv_weight, query_bias, value_bias, proj_weight, proj_bias, second_gain, second_shift, expand_weight, expand_bias, shrink_weight, shrink_bias, cotangent):
    floats = tuple((a.astype(jnp.float32) for a in (tokens, first_gain, first_shift, qkv_weight, query_bias, value_bias, proj_weight, proj_bias, second_gain, second_shift, expand_weight, expand_bias, shrink_weight, shrink_bias)))

    def run_layer(*inputs):
        return layer_forward(*inputs, seq_lengths)
    output, pullback = jax.vjp(run_layer, *floats)
    gradients = pullback(cotangent.astype(jnp.float32))
    return (output.astype(jnp.bfloat16), gradients[0], gradients[1], gradients[2], gradients[3], gradients[4], gradients[5], gradients[6], gradients[7], gradients[8], gradients[9], gradients[10], gradients[11], gradients[12], gradients[13])
```

```python
import functools
import math

import jax
import jax.numpy as jnp
from jax import lax
from jax.experimental import pallas as pl
from jax.experimental.pallas import tpu as pltpu
from jax.sharding import PartitionSpec as P

f32 = jnp.float32
bf16 = jnp.bfloat16
MESH = pl.DeviceIdType.MESH
ANY = pl.BlockSpec(memory_space=pl.ANY)
VMEM = pl.BlockSpec(memory_space=pltpu.VMEM)
SMEM = pl.BlockSpec(memory_space=pltpu.SMEM)

H = 12
epsilon = 1e-05
masked_score = -1e30
ROWS = 1024
SWAP = 768
D = 768
FF = 3072
PAIRS = 6
BLK = 256
DEST = 32
VMEM_LIMIT = 63 * 2**20
GELU_C = 0.7978845608028654


def nn(a, b):
    return lax.dot_general(a, b, (((1,), (0,)), ((), ())), preferred_element_type=f32)


def nt(a, b):
    return lax.dot_general(a, b, (((1,), (1,)), ((), ())), preferred_element_type=f32)


def row_stats(v):
    mean = jnp.mean(v, axis=-1, keepdims=True)
    centered = v - mean
    var = jnp.mean(centered * centered, axis=-1, keepdims=True)
    return centered * lax.rsqrt(var + epsilon), lax.rsqrt(var + epsilon)


def lane_ids(shape):
    return lax.broadcasted_iota(jnp.int32, shape, 1)


def row_ids(shape):
    return lax.broadcasted_iota(jnp.int32, shape, 0)


def split3(v):
    hi = v.astype(bf16).astype(f32)
    rest = v - hi
    mid = rest.astype(bf16).astype(f32)
    return hi, mid, rest - mid


def rotated(m, shift, i):
    coarse = lax.shift_right_logical(shift, 8)
    fine = lax.bitwise_and(shift, 255)

    def two(k):
        blocks = [m[pl.ds(pl.multiple_of(((i + k + n) % 4) * BLK, BLK), BLK), :] for n in range(2)]
        return jnp.concatenate(blocks, axis=0)

    part = jnp.where(coarse == 1, two(1), jnp.where(coarse == 2, two(2), two(3)))
    shape = (BLK, 2 * BLK)
    pick = (lane_ids(shape) == row_ids(shape) + fine).astype(f32).astype(bf16)
    return nn(pick, part)


def forward_kernel(
    lens, tok_h, cot_h, gain1, shift1, wq_h, qb, vb, wp_h, pb, gain2, shift2,
    x_h, cotr_h, n1_h, qx_h, kx_h, v_h, ctx_h, mid_h, n2_h,
    tok, cot, tok_in, cot_in, dbl, x, cotr, n1, qx, kx, v, ctx, mid, n2, wq, wp,
    load_sem, send_sem, recv_sem, out_sem,
):
    b = lax.axis_index("batch")
    c = lax.axis_index("seq")
    partner = (b, 1 - c)
    a = lens[0, 0]
    loads = [
        pltpu.make_async_copy(src, dst, load_sem.at[i])
        for i, (src, dst) in enumerate(((tok_h, tok), (wq_h, wq), (cot_h, cot), (wp_h, wp)))
    ]
    for cp in loads:
        cp.start()
    barrier = pltpu.get_barrier_semaphore()
    pl.semaphore_signal(barrier, inc=1, device_id=partner, device_id_type=MESH)
    pl.semaphore_wait(barrier, 1)
    swaps = [
        pltpu.make_async_remote_copy(
            src_ref=src.at[pl.ds(0, SWAP)], dst_ref=dst, send_sem=send_sem.at[i],
            recv_sem=recv_sem.at[i], device_id=partner, device_id_type=MESH)
        for i, (src, dst) in enumerate(((tok_h, tok_in), (cot_h, cot_in)))
    ]
    for cp in swaps:
        cp.start()

    def merged(own, other, r):
        m = own[pl.ds(r, BLK), :].astype(f32)
        o = other[pl.ds(r, BLK), :].astype(f32)
        return jnp.where(row_ids((BLK, D)) + r >= a, m, o)

    def fill(own, other):
        def step(i, _):
            r = pl.multiple_of(i * BLK, BLK)
            dbl[pl.ds(r, BLK), :] = merged(own, other, r).astype(bf16)
            return 0
        lax.fori_loop(0, SWAP // BLK, step, 0)
        dbl[SWAP:ROWS, :] = own[SWAP:ROWS, :]

    loads[0].wait()
    swaps[0].wait()
    fill(tok, tok_in)
    loads[1].wait()

    lane = lane_ids((BLK, 128))
    bound = jnp.where(c == 0, 0, ROWS - a)

    def project(i, _):
        r = pl.multiple_of(i * BLK, BLK)
        rows = pl.ds(r, BLK)
        xt = rotated(dbl, a, i)
        x[rows, :] = xt.astype(bf16)
        normed, _unused = row_stats(xt)
        nt_ = (normed * gain1[...].reshape(1, D) + shift1[...].reshape(1, D)).astype(bf16)
        n1[rows, :] = nt_
        late = row_ids((BLK, 128)) + r >= bound
        q_flag = jnp.where(late, 1.0, 0.0).astype(f32)
        k_flag = jnp.where(late, 0.0, masked_score).astype(f32)
        q = nn(nt_, wq[:, 0:D]) + qb[...].reshape(1, D)
        q = q.astype(bf16).astype(f32) * 0.125
        k = nn(nt_, wq[:, D : 2 * D])
        vv = nn(nt_, wq[:, 2 * D : 3 * D]) + vb[...].reshape(1, D)
        v[rows, :] = vv.astype(bf16)
        for p in range(PAIRS):
            qp = q[:, 128 * p : 128 * p + 128]
            kp = k[:, 128 * p : 128 * p + 128]
            for s in range(2):
                mine = lane < 64 if s == 0 else lane >= 64
                base = 64 if s == 0 else 0
                q_aug = jnp.where(lane == base, q_flag, 0.0)
                k_aug = jnp.where(lane == base, k_flag, 1.0)
                k_aug = jnp.where(lane > base + 3, 0.0, k_aug)
                at = 256 * p + 128 * s
                qx[rows, at : at + 128] = jnp.where(mine, qp, q_aug).astype(bf16)
                kx[rows, at : at + 128] = jnp.where(mine, kp, k_aug).astype(bf16)
        return 0

    lax.fori_loop(0, ROWS // BLK, project, 0)
    early = [
        pltpu.make_async_copy(src, dst, out_sem.at[i])
        for i, (src, dst) in enumerate(((x, x_h), (n1, n1_h), (kx, kx_h), (v, v_h)))
    ]
    for cp in early:
        cp.start()

    causal = lane_ids((BLK, BLK)) <= row_ids((BLK, BLK))

    def attend(p, _):
        at = pl.multiple_of(p * 256, 256)
        vat = pl.multiple_of(p * 128, 128)
        for i in range(ROWS // BLK):
            rows = slice(BLK * i, BLK * i + BLK)
            outs = []
            for s in range(2):
                cols = pl.ds(at + 128 * s, 128)
                mine = lane < 64 if s == 0 else lane >= 64
                base = 64 if s == 0 else 0
                qt = qx[rows, cols]
                diag = jnp.where(causal, nt(qt, kx[rows, cols]), masked_score)
                peak = jnp.max(diag, axis=-1, keepdims=True)
                if i > 0:
                    full = nt(qt, kx[0 : BLK * i, cols])
                    peak = jnp.maximum(peak, jnp.max(full, axis=-1, keepdims=True))
                vd = v[rows, pl.ds(vat, 128)]
                vd = jnp.where(mine, vd, jnp.ones_like(vd))
                o = nn(jnp.exp(diag - peak).astype(bf16), vd)
                if i > 0:
                    vf = v[0 : BLK * i, pl.ds(vat, 128)]
                    lf = lane_ids((BLK * i, 128))
                    vf = jnp.where(lf < 64 if s == 0 else lf >= 64, vf, jnp.ones_like(vf))
                    o = o + nn(jnp.exp(full - peak).astype(bf16), vf)
                outs.append(o / pltpu.roll(o, 64, 1))
                hi, mid_, lo = split3(-(peak + jnp.log(o)))
                qn = jnp.where(lane == base + 1, hi, qt.astype(f32))
                qn = jnp.where(lane == base + 2, mid_, qn)
                qn = jnp.where(lane == base + 3, lo, qn)
                qx[rows, cols] = qn.astype(bf16)
            ctx[rows, pl.ds(vat, 128)] = jnp.where(lane < 64, outs[0], outs[1]).astype(bf16)
        return 0

    lax.fori_loop(0, PAIRS, attend, 0)
    loads[3].wait()

    def finish(i, _):
        r = pl.multiple_of(i * BLK, BLK)
        rows = pl.ds(r, BLK)
        m = nn(ctx[rows, :], wp[...]) + pb[...].reshape(1, D) + x[rows, :].astype(f32)
        mid[rows, :] = m
        normed, _unused = row_stats(m)
        n2[rows, :] = (normed * gain2[...].reshape(1, D) + shift2[...].reshape(1, D)).astype(bf16)
        return 0

    lax.fori_loop(0, ROWS // BLK, finish, 0)
    late_out = [
        pltpu.make_async_copy(src, dst, out_sem.at[4 + i])
        for i, (src, dst) in enumerate(((qx, qx_h), (ctx, ctx_h), (mid, mid_h), (n2, n2_h)))
    ]
    for cp in late_out:
        cp.start()
    loads[2].wait()
    swaps[1].wait()
    fill(cot, cot_in)

    def turn(i, _):
        r = pl.multiple_of(i * BLK, BLK)
        cotr[pl.ds(r, BLK), :] = rotated(dbl, a, i).astype(bf16)
        return 0

    lax.fori_loop(0, ROWS // BLK, turn, 0)
    last = pltpu.make_async_copy(cotr, cotr_h, out_sem.at[8])
    last.start()
    for cp in early + late_out + [last]:
        cp.wait()


def forward_call(lens, tok, cot, gain1, shift1, wq, qb, vb, wp, pb, gain2, shift2):
    shapes = [
        ((ROWS, D), bf16),
        ((ROWS, D), bf16),
        ((ROWS, D), bf16),
        ((ROWS, 2 * D), bf16),
        ((ROWS, 2 * D), bf16),
        ((ROWS, D), bf16),
        ((ROWS, D), bf16),
        ((ROWS, D), f32),
        ((ROWS, D), bf16),
    ]
    x, cotr, n1, qx, kx, v, ctx, mid, n2 = [pltpu.VMEM(s, t) for s, t in shapes]
    return pl.pallas_call(
        forward_kernel,
        out_shape=[jax.ShapeDtypeStruct(s, t) for s, t in shapes],
        in_specs=[SMEM, ANY, ANY, VMEM, VMEM, ANY, VMEM, VMEM, ANY, VMEM, VMEM, VMEM],
        out_specs=[ANY] * 9,
        scratch_shapes=[
            pltpu.VMEM((ROWS, D), bf16), pltpu.VMEM((ROWS, D), bf16),
            pltpu.VMEM((SWAP, D), bf16), pltpu.VMEM((SWAP, D), bf16),
            pltpu.VMEM((ROWS, D), bf16),
            x, cotr, n1, qx, kx, v, ctx, mid, n2,
            pltpu.VMEM((D, 3 * D), bf16), pltpu.VMEM((D, D), bf16),
            pltpu.SemaphoreType.DMA((4,)), pltpu.SemaphoreType.DMA((2,)),
            pltpu.SemaphoreType.DMA((2,)), pltpu.SemaphoreType.DMA((9,)),
        ],
        compiler_params=pltpu.CompilerParams(
            collective_id=0, has_side_effects=True, vmem_limit_bytes=VMEM_LIMIT),
        cost_estimate=pl.CostEstimate(
            flops=14 * 10**9, bytes_accessed=30 * 10**6, transcendentals=8 * 10**6),
        name="forward",
    )(lens, tok, cot, gain1, shift1, wq, qb, vb, wp, pb, gain2, shift2)


def norm_back(v, gain, r):
    n, scale = row_stats(v)
    u = gain * r
    back = scale * (u - jnp.mean(u, axis=-1, keepdims=True) - n * jnp.mean(u * n, axis=-1, keepdims=True))
    return back, jnp.sum(r * n, axis=0, keepdims=True), jnp.sum(r, axis=0, keepdims=True)


def backward_kernel(
    nz, direct,
    lens, x_h, cot_h, n1_h, qx_h, kx_h, v_h, ctx_h, mid_h, n2_h,
    gain1, gain2, eb, sb, we_h, ws_h, wq_h, wp_h,
    *rest,
):
    n_out = 7 if direct else 5
    out_h, ig_h, vec_h = rest[:3]
    grads_h = rest[3:n_out]
    (gs, ge, cot, acc, dn, obuf, obuf_in, ibuf, ibuf_in, qx, kx, v, vec, vec_in, load_sem, out_sem,
     swap_send, swap_recv) = rest[n_out : n_out + 18]
    if direct:
        (r0s, r0e, r1s, r1e, r2s, r2e, r3s, r3e, oq, op, oe, os_,
         s_send, s_recv, e_send, e_recv, j_send, j_recv, v_send, v_recv) = rest[n_out + 18 :]
    b = lax.axis_index("batch")
    c = lax.axis_index("seq")
    a = lens[0, 0]
    xx = b % 2
    yy = (b // 2) % 2
    zz = b // 4
    partner = (b, 1 - c)
    xn = (b + 1 - 2 * xx, c)
    yn = (b + 2 - 4 * yy, c)
    n1st = (b + (1 - c) * (1 - 2 * xx) + c * (2 - 4 * yy), c)
    n2nd = (b + c * (1 - 2 * xx) + (1 - c) * (2 - 4 * yy), c)
    zpeers = [(zz + i) % nz for i in range(1, nz)] if direct else []
    keep = [(1 - c) * (2 * k + xx) + c * (2 * yy + k) for k in range(2)]
    give = [(1 - c) * (2 * k + 1 - xx) + c * (2 * (1 - yy) + k) for k in range(2)]
    give2 = (1 - c) * (2 * (1 - yy) + xx) + c * (2 * yy + 1 - xx)
    home = 2 * yy + xx
    friends = [partner]
    if direct:
        friends += [xn, yn] + [(b % 4 + 4 * z, c) for z in zpeers]

    def load(src, dst, i):
        return pltpu.make_async_copy(src, dst, load_sem.at[i])

    def remote(src, dst, send, recv, to):
        return pltpu.make_async_remote_copy(
            src_ref=src, dst_ref=dst, send_sem=send, recv_sem=recv,
            device_id=to, device_id_type=MESH)

    def copies(kind, u, stage):
        slot = u % 2
        if kind == "s":
            if stage == 0:
                return [remote(gs.at[1 - c, :, u], r0s.at[slot], s_send.at[u, 0], s_recv.at[u, 0], partner)]
            if stage == 1:
                return [remote(gs.at[c, give[k], u], r1s.at[slot, k], s_send.at[u, 1 + k], s_recv.at[u, 1 + k], n1st)
                        for k in range(2)]
            if stage == 2:
                return [remote(gs.at[c, give2, u], r2s.at[slot], s_send.at[u, 3], s_recv.at[u, 3], n2nd)]
            return [remote(gs.at[c, home, z], r3s.at[i], j_send.at[i], j_recv.at[i], (b % 4 + 4 * z, c))
                    for i, z in enumerate(zpeers)]
        if stage == 0:
            return [remote(ge.at[u, 1 - c], r0e.at[slot], e_send.at[u, 0], e_recv.at[u, 0], partner)]
        if stage == 1:
            return [remote(ge.at[u, c, give[k]], r1e.at[slot, k], e_send.at[u, 1 + k], e_recv.at[u, 1 + k], n1st)
                    for k in range(2)]
        if stage == 2:
            return [remote(ge.at[u, c, give2], r2e.at[slot], e_send.at[u, 3], e_recv.at[u, 3], n2nd)]
        return [remote(ge.at[u, c, home, z], r3e.at[u, i], e_send.at[u, 4 + i], e_recv.at[u, 4 + i],
                       (b % 4 + 4 * z, c)) for i, z in enumerate(zpeers)]

    def start(kind, u, stage):
        if direct:
            for cp in copies(kind, u, stage):
                cp.start()

    def finish(kind, u, stage):
        for cp in copies(kind, u, stage):
            cp.wait()

    def add_into(dst, src):
        dst[...] = (dst[...].astype(f32) + src[...].astype(f32)).astype(bf16)

    def advance(kind, u, stage):
        finish(kind, u, stage - 1)
        slot = u % 2
        if kind == "s":
            if stage == 1:
                for k in range(4):
                    add_into(gs.at[c, k, u], r0s.at[slot, k])
            elif stage == 2:
                for k in range(2):
                    add_into(gs.at[c, keep[k], u], r1s.at[slot, k])
            elif stage == 3:
                add_into(gs.at[c, home, u], r2s.at[slot])
        else:
            if stage == 1:
                for k in range(4):
                    add_into(ge.at[u, c, k], r0e.at[slot, k])
            elif stage == 2:
                for k in range(2):
                    add_into(ge.at[u, c, keep[k]], r1e.at[slot, k])
            elif stage == 3:
                add_into(ge.at[u, c, home], r2e.at[slot])
        if kind == "e" or stage < 3:
            start(kind, u, stage)

    def settle(kind, u):
        finish(kind, u, 3)
        if kind == "s":
            total = gs[c, home, zz].astype(f32)
            for i in range(nz - 1):
                total = total + r3s[i].astype(f32)
            os_[...] = total
            return
        total = ge[u, c, home, zz].astype(f32)
        for i in range(nz - 1):
            total = total + r3e[u, i].astype(f32)
        for h in range(2):
            half = total[24 * h : 24 * h + 24, :]
            if u < 4:
                oe[:, 768 * u + 384 * h : 768 * u + 384 * h + 384] = half
            elif u == 4:
                op[:, 384 * h : 384 * h + 384] = half
            else:
                for w in range(3):
                    at = 768 * w + 256 * (u - 5) + 128 * h
                    oq[:, at : at + 128] = half[:, 128 * w : 128 * w + 128]

    plan = {}
    for j in range(4):
        plan.setdefault(j + 1, []).extend([(1, "s", j), (1, "e", j)])
        plan.setdefault(j + 2, []).extend([(2, "s", j), (2, "e", j)])
        plan.setdefault(j + 3, []).extend([(3, "s", j), (3, "e", j)])
        plan.setdefault(j + 4, []).append((4, "e", j))
    plan.setdefault(7, []).append((5, "s", 0))
    plan.setdefault(9, []).append((6, "s", 0))
    for u, t in ((4, 4), (5, 6), (6, 8), (7, 10)):
        for stage in range(1, 5):
            plan.setdefault(t + stage, []).append((stage, "e", u))

    def tick(t, now=None):
        if not direct:
            return

        def act():
            for stage, kind, u in sorted(plan.get(t, []), key=lambda e: -e[0]):
                if stage == 6 or (stage == 4 and kind == "e"):
                    settle(kind, u)
                elif stage == 5:
                    start("s", 0, 3)
                else:
                    advance(kind, u, stage)

        if plan.get(t):
            if now is None:
                act()
            else:
                pl.when(now == t)(act)

    barrier = pltpu.get_barrier_semaphore()
    for f in friends:
        pl.semaphore_signal(barrier, inc=1, device_id=f, device_id_type=MESH)
    first = [load(cot_h, cot, 0), load(mid_h, acc, 1), load(qx_h, qx, 2), load(kx_h, kx, 3), load(v_h, v, 4)]
    pl.semaphore_wait(barrier, len(friends))
    vec[...] = jnp.zeros_like(vec)
    chunk = FF // 4

    def feed_forward(we, ws, n2, n2t, at, de):
        own = [load(n2_h, n2, 5), load(we_h, we, 6), load(ws_h, ws, 7)]
        for cp in own + first:
            cp.start()
        own[0].wait()

        def turn(i, _):
            r = pl.multiple_of(i * BLK, BLK)
            n2t[:, pl.ds(r, BLK)] = n2[pl.ds(r, BLK), :].T
            return 0

        lax.fori_loop(0, ROWS // BLK, turn, 0)
        for cp in own[1:] + first[:2]:
            cp.wait()

        def one(j, _):
            cols = pl.ds(pl.multiple_of(j * chunk, chunk), chunk)

            def tile(t, bias_sum):
                r = pl.multiple_of(t * BLK, BLK)
                rows = pl.ds(r, BLK)
                e = nn(n2[rows, :], we[:, cols]) + eb[cols].reshape(1, chunk)
                sq = e * e
                th = jnp.tanh(GELU_C * e * (1.0 + 0.044715 * sq))
                half = 0.5 * (1.0 + th)
                low = (e * half).astype(bf16)
                slope = half + (0.5 * GELU_C) * e * (1.0 - th * th) * (1.0 + (3 * 0.044715) * sq)
                grad = (nt(cot[rows, :], ws[cols, :]) * slope).astype(bf16)
                at[:, rows] = low.T
                de[rows, :] = grad
                acc[rows, :] += nn(low, ws[cols, :])
                part = nt(grad, we[:, cols])
                dn[rows, :] = jnp.where(j == 0, part, dn[rows, :] + part)
                return bias_sum + jnp.sum(grad.astype(f32), axis=0, keepdims=True)

            bias_sum = lax.fori_loop(0, ROWS // BLK, tile, jnp.zeros((1, chunk), f32))
            vec[pl.ds(8 + j, 1), :] = bias_sum
            for t in range(1, 4):
                tick(t, j)

            def shrink_part(i, _):
                r = pl.multiple_of(i * 192, 64)
                g = nn(at[pl.ds(r, 192), :], cot[...]).astype(bf16)
                for h in range(2):
                    gs[h, i, j] = g[96 * h : 96 * h + 96, :]
                return 0

            lax.fori_loop(0, 4, shrink_part, 0)
            start("s", j, 0)

            def expand_part(i, _):
                r = pl.multiple_of(i * 192, 64)
                g = nn(n2t[pl.ds(r, 192), :], de[...])
                for w in range(8):
                    q = g[24 * w : 24 * w + 24, :]
                    q = jnp.concatenate([q[:, 0:384], q[:, 384:768]], axis=0).astype(bf16)
                    ge[j, w % 2, w // 2, i] = q
                return 0

            lax.fori_loop(0, 4, expand_part, 0)
            start("e", j, 0)
            return 0

        lax.fori_loop(0, 4, one, 0)

    pl.run_scoped(
        feed_forward, pltpu.VMEM((D, FF), bf16), pltpu.VMEM((FF, D), bf16), pltpu.VMEM((ROWS, D), bf16),
        pltpu.VMEM((D, ROWS), bf16), pltpu.VMEM((chunk, ROWS), bf16), pltpu.VMEM((ROWS, chunk), bf16))
    tick(4)

    def unroll(dbl, buf):
        def step(i, _):
            r = pl.multiple_of(i * BLK, BLK)
            buf[pl.ds(r, BLK), :] = rotated(dbl, ROWS - a, i).astype(bf16)
            return 0

        lax.fori_loop(0, ROWS // BLK, step, 0)

    out_swap = remote(obuf.at[pl.ds(0, SWAP)], obuf_in, swap_send.at[0], swap_recv.at[0], partner)
    ig_swap = remote(ibuf.at[pl.ds(0, SWAP)], ibuf_in, swap_send.at[1], swap_recv.at[1], partner)
    lane = lane_ids((BLK, 128))

    def middle(dox):
        def second(mid, ctx, wp, dbl, gat):
            own = [load(mid_h, mid, 5), load(ctx_h, ctx, 6), load(wp_h, wp, 7)]
            for cp in own:
                cp.start()
            for cp in own:
                cp.wait()

            def tile(i, sums):
                r = pl.multiple_of(i * BLK, BLK)
                rows = pl.ds(r, BLK)
                dbl[rows, :] = (acc[rows, :] + sb[...].reshape(1, D)).astype(bf16)
                back, dgain, dshift = norm_back(mid[rows, :], gain2[...].reshape(1, D), dn[rows, :])
                ct = cot[rows, :].astype(f32)
                dmid = ct + back
                dn[rows, :] = dmid
                ga = dmid.astype(bf16)
                gat[rows, :] = ga
                dc = nt(ga, wp[...]).astype(bf16).astype(f32)
                cx = ctx[rows, :].astype(f32)
                for p in range(PAIRS):
                    d = dc[:, 128 * p : 128 * p + 128]
                    prod = d * cx[:, 128 * p : 128 * p + 128]
                    for s in range(2):
                        mine = lane < 64 if s == 0 else lane >= 64
                        base = 64 if s == 0 else 0
                        inner = jnp.sum(jnp.where(mine, prod, 0.0), axis=-1, keepdims=True)
                        hi, mid_, lo = split3(-inner)
                        aug = jnp.where(lane == base, hi, 0.0)
                        aug = jnp.where(lane == base + 1, mid_, aug)
                        aug = jnp.where(lane == base + 2, lo, aug)
                        at = 256 * p + 128 * s
                        dox[rows, at : at + 128] = jnp.where(mine, d, aug).astype(bf16)
                dpb = jnp.sum(ga.astype(f32), axis=0, keepdims=True)
                dsb = jnp.sum(ct, axis=0, keepdims=True)
                return tuple(o + n for o, n in zip(sums, (dgain, dshift, dpb, dsb)))

            zero = jnp.zeros((1, D), f32)
            sums = lax.fori_loop(0, ROWS // BLK, tile, (zero,) * 4)
            for at, s in zip((5, 6, 4, 7), sums):
                vec[at : at + 1, :] = s
            unroll(dbl, obuf)
            out_swap.start()

            def proj_part(i, _):
                r = pl.multiple_of(i * 192, 64)
                g = lax.dot_general(ctx[:, pl.ds(pl.multiple_of(i * 384, 128), 384)], gat[...],
                                    (((0,), (0,)), ((), ())), preferred_element_type=f32)
                for w in range(16):
                    q = g[24 * w : 24 * w + 24, :]
                    q = jnp.concatenate([q[:, 0:384], q[:, 384:768]], axis=0).astype(bf16)
                    ge[4, w % 2, (w // 2) % 4, 2 * i + w // 8] = q
                return 0

            lax.fori_loop(0, 2, proj_part, 0)
            start("e", 4, 0)

        pl.run_scoped(
            second, pltpu.VMEM((ROWS, D), f32), pltpu.VMEM((ROWS, D), bf16), pltpu.VMEM((D, D), bf16),
            pltpu.VMEM((ROWS, D), bf16), pltpu.VMEM((ROWS, D), bf16))
        return dox

    triangle = row_ids((BLK, BLK)) <= lane_ids((BLK, BLK))

    def attention(dox, dqkv, n1t, wq, x):
        later = [load(wq_h, wq, 5), load(x_h, x, 6)]
        for cp in later:
            cp.start()

        def attention_loop(n1, ktr, dqt):
            ln1 = load(n1_h, n1, 7)
            ln1.start()
            for cp in first[2:]:
                cp.wait()
            ln1.wait()

            def turn(i, _):
                r = pl.multiple_of(i * BLK, BLK)
                n1t[:, pl.ds(r, BLK)] = n1[pl.ds(r, BLK), :].T
                return 0

            lax.fori_loop(0, ROWS // BLK, turn, 0)

            def pair(p, _):
                at = pl.multiple_of(p * 256, 256)
                pat = pl.multiple_of(p * 128, 128)
                lf = lane_ids((ROWS, 128))
                kp = jnp.where(lf < 64, kx[:, pl.ds(at, 128)], kx[:, pl.ds(at + 128, 128)])
                ktr[...] = kp.T
                dqt[...] = jnp.zeros_like(dqt)
                dv_sum = jnp.zeros((1, 128), f32)
                for kb in range(ROWS // BLK):
                    krows = slice(BLK * kb, BLK * kb + BLK)
                    dks, dvs = [], []
                    for s in range(2):
                        cols = pl.ds(at + 128 * s, 128)
                        mine = lane < 64 if s == 0 else lane >= 64
                        vd = v[krows, pl.ds(pat, 128)]
                        vd = jnp.where(mine, vd, jnp.ones_like(vd))
                        kd = kx[krows, cols]
                        dk = jnp.zeros((BLK, 128), f32)
                        dv = jnp.zeros((BLK, 128), f32)
                        for qi in range(kb, ROWS // BLK):
                            qrows = slice(BLK * qi, BLK * qi + BLK)
                            qt = qx[qrows, cols]
                            dt = dox[qrows, cols]
                            prob = jnp.exp(nt(kd, qt))
                            if qi == kb:
                                prob = jnp.where(triangle, prob, 0.0)
                            ds = (prob * nt(vd, dt)).astype(bf16)
                            dv = dv + nn(prob.astype(bf16), dt)
                            dk = dk + nn(ds, qt)
                            dqt[64 * s : 64 * s + 64, qrows] += nn(ktr[64 * s : 64 * s + 64, krows], ds)
                        dks.append(dk)
                        dvs.append(dv)
                    dqkv[krows, pl.ds(D + pat, 128)] = jnp.where(lane < 64, dks[0], dks[1]).astype(bf16)
                    dvp = jnp.where(lane < 64, dvs[0], dvs[1]).astype(bf16)
                    dqkv[krows, pl.ds(2 * D + pat, 128)] = dvp
                    dv_sum = dv_sum + jnp.sum(dvp.astype(f32), axis=0, keepdims=True)
                dq = (dqt[...] * 0.125).astype(bf16).T
                dqkv[:, pl.ds(pat, 128)] = dq
                vec[2:3, pl.ds(pat, 128)] = jnp.sum(dq.astype(f32), axis=0, keepdims=True)
                vec[3:4, pl.ds(pat, 128)] = dv_sum
                for t in range(5, 11):
                    tick(t, p + 5)

                @pl.when(p % 2 == 1)
                def _():
                    k = p // 2

                    def qkv_part(i, _):
                        r = pl.multiple_of(i * 384, 128)
                        for w in range(3):
                            g = nn(n1t[pl.ds(r, 384), :], dqkv[:, pl.ds(pl.multiple_of(768 * w + 256 * k, 256), 256)])
                            for q_ in range(16):
                                q = g[24 * q_ : 24 * q_ + 24, :]
                                q = jnp.concatenate([q[:, 0:128], q[:, 128:256]], axis=0).astype(bf16)
                                ge[5 + k, q_ % 2, (q_ // 2) % 4, 2 * i + q_ // 8, :, 128 * w : 128 * w + 128] = q
                        return 0

                    lax.fori_loop(0, 2, qkv_part, 0)
                    start("e", 5 + k, 0)

                return 0

            lax.fori_loop(0, PAIRS, pair, 0)

        pl.run_scoped(
            attention_loop, pltpu.VMEM((ROWS, D), bf16), pltpu.VMEM((128, ROWS), bf16), pltpu.VMEM((128, ROWS), f32))
        for cp in later:
            cp.wait()

        def tail(dbl):
            def tile(i, sums):
                r = pl.multiple_of(i * BLK, BLK)
                rows = pl.ds(r, BLK)
                g = nt(dqkv[rows, :], wq[...])
                back, dgain, dshift = norm_back(x[rows, :].astype(f32), gain1[...].reshape(1, D), g)
                dbl[rows, :] = (dn[rows, :] + back).astype(bf16)
                for t in range(11, 15):
                    tick(t, i + 11)
                return sums[0] + dgain, sums[1] + dshift

            zero = jnp.zeros((1, D), f32)
            sums = lax.fori_loop(0, ROWS // BLK, tile, (zero,) * 2)
            vec[0:1, :] = sums[0]
            vec[1:2, :] = sums[1]
            unroll(dbl, ibuf)
            ig_swap.start()

        pl.run_scoped(tail, pltpu.VMEM((ROWS, D), bf16))

    def both(dox):
        middle(dox)
        pl.run_scoped(
            functools.partial(attention, dox), pltpu.VMEM((ROWS, 3 * D), bf16), pltpu.VMEM((D, ROWS), bf16),
            pltpu.VMEM((D, 3 * D), bf16), pltpu.VMEM((ROWS, D), bf16))

    pl.run_scoped(both, pltpu.VMEM((ROWS, 2 * D), bf16))

    outs = []

    def emit(src, dst):
        cp = pltpu.make_async_copy(src, dst, out_sem.at[len(outs)])
        cp.start()
        outs.append(cp)

    if direct:
        at = 0
        for group in ([partner], [xn], [yn], [(b % 4 + 4 * z, c) for z in zpeers]):
            cps = [remote(vec, vec_in.at[at + i], v_send.at[at + i], v_recv.at[at + i], to)
                   for i, to in enumerate(group)]
            for cp in cps:
                cp.start()
            for cp in cps:
                cp.wait()
            total = vec[...]
            for i in range(len(group)):
                total = total + vec_in[at + i]
            vec[...] = total
            at += len(group)
        emit(vec, vec_h)
        for src, dst in zip((oq, op, oe, os_), grads_h):
            emit(src, dst)
    else:
        emit(vec, vec_h)
        emit(gs, grads_h[0])
        emit(ge, grads_h[1])

    def give_back(swap, buf, buf_in, final):
        swap.wait()

        def step(i, _):
            r = pl.multiple_of(i * BLK, BLK)
            rows = pl.ds(r, BLK)
            own = buf[rows, :].astype(f32)
            other = buf_in[rows, :].astype(f32)
            final[rows, :] = jnp.where(row_ids((BLK, D)) + r >= a, own, other).astype(final.dtype)
            return 0

        lax.fori_loop(0, SWAP // BLK, step, 0)
        final[SWAP:ROWS, :] = buf[SWAP:ROWS, :].astype(final.dtype)

    give_back(out_swap, obuf, obuf_in, cot)
    emit(cot, out_h)
    give_back(ig_swap, ibuf, ibuf_in, acc)
    emit(acc, ig_h)
    for cp in outs:
        cp.wait()


def backward_call(nz, direct, *args):
    unit = (48, 384)
    if direct:
        grads = [((24, 3 * D), f32), ((24, D), f32), ((24, FF), f32), ((96, D), f32)]
    else:
        grads = [((2, 4, 4, 96, D), bf16), ((8, 2, 4, 4) + unit, bf16)]
    shapes = [((ROWS, D), bf16), ((ROWS, D), f32), ((16, D), f32)] + grads
    scratch = [
        pltpu.VMEM((2, 4, 4, 96, D), bf16), pltpu.VMEM((8, 2, 4, 4) + unit, bf16),
        pltpu.VMEM((ROWS, D), bf16), pltpu.VMEM((ROWS, D), f32), pltpu.VMEM((ROWS, D), f32),
        pltpu.VMEM((ROWS, D), bf16), pltpu.VMEM((SWAP, D), bf16),
        pltpu.VMEM((ROWS, D), bf16), pltpu.VMEM((SWAP, D), bf16),
        pltpu.VMEM((ROWS, 2 * D), bf16), pltpu.VMEM((ROWS, 2 * D), bf16), pltpu.VMEM((ROWS, D), bf16),
        pltpu.VMEM((16, D), f32), pltpu.VMEM((6, 16, D), f32),
        pltpu.SemaphoreType.DMA((8,)), pltpu.SemaphoreType.DMA((8,)),
        pltpu.SemaphoreType.DMA((2,)), pltpu.SemaphoreType.DMA((2,)),
    ]
    if direct:
        scratch += [
            pltpu.VMEM((2, 4, 96, D), bf16), pltpu.VMEM((2, 4, nz) + unit, bf16),
            pltpu.VMEM((2, 2, 96, D), bf16), pltpu.VMEM((2, 2, nz) + unit, bf16),
            pltpu.VMEM((2, 96, D), bf16), pltpu.VMEM((2, nz) + unit, bf16),
            pltpu.VMEM((nz - 1, 96, D), bf16), pltpu.VMEM((8, nz - 1) + unit, bf16),
            pltpu.VMEM((24, 3 * D), f32), pltpu.VMEM((24, D), f32), pltpu.VMEM((24, FF), f32), pltpu.VMEM((96, D), f32),
            pltpu.SemaphoreType.DMA((4, 4)), pltpu.SemaphoreType.DMA((4, 4)),
            pltpu.SemaphoreType.DMA((8, 7)), pltpu.SemaphoreType.DMA((8, 7)),
            pltpu.SemaphoreType.DMA((3,)), pltpu.SemaphoreType.DMA((3,)),
            pltpu.SemaphoreType.DMA((6,)), pltpu.SemaphoreType.DMA((6,)),
        ]
    return pl.pallas_call(
        functools.partial(backward_kernel, nz, direct),
        out_shape=[jax.ShapeDtypeStruct(s, t) for s, t in shapes],
        in_specs=[SMEM] + [ANY] * 9 + [VMEM] * 4 + [ANY] * 4,
        out_specs=[ANY] * len(shapes),
        scratch_shapes=scratch,
        compiler_params=pltpu.CompilerParams(
            collective_id=1, has_side_effects=True, vmem_limit_bytes=VMEM_LIMIT),
        cost_estimate=pl.CostEstimate(
            flops=50 * 10**9, bytes_accessed=50 * 10**6, transcendentals=12 * 10**6),
        name="backward",
    )(*args)


def on_device(nz, direct, tokens, lens, gain1, shift1, wq, qb, vb, wp, pb, gain2, shift2, we, eb, ws, sb, cot):
    x, cotr, n1, qx, kx, v, ctx, mid, n2 = forward_call(
        lens, tokens, cot, gain1, shift1, wq, qb, vb, wp, pb, gain2, shift2)
    out, ig, vec, *grads = backward_call(
        nz, direct, lens, x, cotr, n1, qx, kx, v, ctx, mid, n2, gain1, gain2, eb, sb, we, ws, wq, wp)
    shards = lax.axis_size("batch") * 2
    me = lax.axis_index("batch") * 2 + lax.axis_index("seq")

    if direct:
        gq, gp, ge, gs = grads

        def own_part(row, rows=1):
            flat = vec[row : row + rows].reshape(rows * D)
            n = rows * D // shards
            return lax.dynamic_slice(flat, (me * n,), (n,))
    else:
        def scatter(g):
            return lax.psum_scatter(g, ("batch", "seq"), scatter_dimension=0, tiled=True)

        def own_part(row, rows=1):
            return scatter(vec[row : row + rows].reshape(rows * D))

        us, ue = (g.astype(f32) for g in grads)
        gs = scatter(us.transpose(2, 1, 0, 3, 4).reshape(FF, D))
        ue = ue.reshape(8, 2, 4, 4, 2, 24, 384)
        wide = ue[:5].transpose(3, 2, 1, 5, 0, 4, 6).reshape(D, 5 * D)
        ge = scatter(wide[:, :FF])
        gp = scatter(wide[:, FF:])
        gq = ue[5:].reshape(3, 2, 4, 4, 2, 24, 3, 128).transpose(3, 2, 1, 5, 6, 0, 4, 7).reshape(D, 3 * D)
        gq = scatter(gq)
    return (out, ig, own_part(0), own_part(1), gq, own_part(2), own_part(3), gp, own_part(4),
            own_part(5), own_part(6), ge, own_part(8, 4), gs, own_part(7))


def solution(mesh):
    nz = mesh.shape["batch"] // 4
    direct = mesh.shape["batch"] == 16 and mesh.shape["seq"] == 2
    rows = P(("batch", "seq"), None)
    part = P(("batch", "seq"))
    whole = P()
    in_specs = (rows, P("batch", None)) + (whole,) * 13 + (rows,)
    out_specs = (rows, rows, part, part, rows, part, part, rows, part, part, part, rows, part, rows, part)
    return jax.shard_map(
        functools.partial(on_device, nz, direct),
        mesh=mesh, in_specs=in_specs, out_specs=out_specs, check_vma=False)
```

```python
import functools
import math

import jax
import jax.numpy as jnp
from jax import lax
from jax.experimental import pallas as pl
from jax.experimental.pallas import tpu as pltpu
from jax.sharding import PartitionSpec as P

f32 = jnp.float32
bf16 = jnp.bfloat16
MESH = pl.DeviceIdType.MESH
ANY = pl.BlockSpec(memory_space=pl.ANY)
VMEM = pl.BlockSpec(memory_space=pltpu.VMEM)
SMEM = pl.BlockSpec(memory_space=pltpu.SMEM)

H = 12
epsilon = 1e-05
masked_score = -1e30
ROWS = 1024
SWAP = 768
D = 768
FF = 3072
PAIRS = 6
BLK = 256
VMEM_LIMIT = 63 * 2**20
GELU_C = 0.7978845608028654


def nn(a, b):
    return lax.dot_general(a, b, (((1,), (0,)), ((), ())), preferred_element_type=f32)


def nt(a, b):
    return lax.dot_general(a, b, (((1,), (1,)), ((), ())), preferred_element_type=f32)


def tn(a, b):
    return lax.dot_general(a, b, (((0,), (0,)), ((), ())), preferred_element_type=f32)


def row_stats(v):
    mean = jnp.mean(v, axis=-1, keepdims=True)
    centered = v - mean
    var = jnp.mean(centered * centered, axis=-1, keepdims=True)
    return centered * lax.rsqrt(var + epsilon), lax.rsqrt(var + epsilon)


def lane_ids(shape):
    return lax.broadcasted_iota(jnp.int32, shape, 1)


def row_ids(shape):
    return lax.broadcasted_iota(jnp.int32, shape, 0)


def split3(v):
    hi = v.astype(bf16).astype(f32)
    rest = v - hi
    mid = rest.astype(bf16).astype(f32)
    return hi, mid, rest - mid


def rotated(m, shift, i):
    coarse = lax.shift_right_logical(shift, 8)
    fine = lax.bitwise_and(shift, 255)

    def two(k):
        blocks = [m[pl.ds(pl.multiple_of(((i + k + n) % 4) * BLK, BLK), BLK), :] for n in range(2)]
        return jnp.concatenate(blocks, axis=0)

    part = jnp.where(coarse == 1, two(1), jnp.where(coarse == 2, two(2), two(3)))
    shape = (BLK, 2 * BLK)
    pick = (lane_ids(shape) == row_ids(shape) + fine).astype(f32).astype(bf16)
    return nn(pick, part)


def norm_back(v, gain, r):
    n, scale = row_stats(v)
    u = gain * r
    back = scale * (u - jnp.mean(u, axis=-1, keepdims=True) - n * jnp.mean(u * n, axis=-1, keepdims=True))
    return back, jnp.sum(r * n, axis=0, keepdims=True), jnp.sum(r, axis=0, keepdims=True)


def gelu_parts(e):
    sq = e * e
    th = jnp.tanh(e * (GELU_C + (GELU_C * 0.044715) * sq))
    half = 0.5 + 0.5 * th
    slope = half + (e * (1.0 - th * th)) * (0.5 * GELU_C + (1.5 * GELU_C * 0.044715) * sq)
    return e * half, slope


def spare_rows(*rows):
    ids = row_ids((64, rows[0].shape[1]))
    out = jnp.zeros(ids.shape, f32)
    for i, row in enumerate(rows):
        out = jnp.where(ids == i, row, out)
    return out


def with_spare(s, part, spare):
    return jnp.concatenate([part, spare] if s == 0 else [spare, part], axis=0).astype(bf16)


def layer_kernel(
    nz, direct,
    lens, tok_h, cot_h, gain1, shift1, wq_h, qb, vb, wp_h, pb, gain2, shift2, we_h, eb, ws_h, sb,
    *rest,
):
    n_out = 10 if direct else 8
    out_h, out_in_h, ig_h, ig_in_h, vec_h, mid_h = rest[:6]
    grads_h = rest[6:n_out]
    (gs, ge, tok_in, cot_in, m, cot, x, n1, q, qxt, kx, v, ctxt, acc, dn, n2, wq, wp, lse, vec, vec_in,
     load_sem, out_sem, swap_send, swap_recv) = rest[n_out : n_out + 25]
    if direct:
        (r0s, r0e, r1s, r1e, r2s, r2e, r3s, r3e, oq, op, oe, os_,
         s_send, s_recv, e_send, e_recv, j_send, j_recv, v_send, v_recv) = rest[n_out + 25 :]
    b = lax.axis_index("batch")
    c = lax.axis_index("seq")
    a = lens[0, 0]
    xx = b % 2
    yy = (b // 2) % 2
    zz = b // 4
    partner = (b, 1 - c)
    xn = (b + 1 - 2 * xx, c)
    yn = (b + 2 - 4 * yy, c)
    n1st = (b + (1 - c) * (1 - 2 * xx) + c * (2 - 4 * yy), c)
    n2nd = (b + c * (1 - 2 * xx) + (1 - c) * (2 - 4 * yy), c)
    zpeers = [(zz + i) % nz for i in range(1, nz)] if direct else []
    keep = [(1 - c) * (2 * k + xx) + c * (2 * yy + k) for k in range(2)]
    give = [(1 - c) * (2 * k + 1 - xx) + c * (2 * (1 - yy) + k) for k in range(2)]
    give2 = (1 - c) * (2 * (1 - yy) + xx) + c * (2 * yy + 1 - xx)
    home = 2 * yy + xx
    friends = [partner]
    if direct:
        friends += [xn, yn] + [(b % 4 + 4 * z, c) for z in zpeers]

    def load(src, dst, i):
        return pltpu.make_async_copy(src, dst, load_sem.at[i])

    def remote(src, dst, send, recv, to):
        return pltpu.make_async_remote_copy(
            src_ref=src, dst_ref=dst, send_sem=send, recv_sem=recv,
            device_id=to, device_id_type=MESH)

    def place(u):
        return u if not direct else u % 5

    def copies(kind, u, stage):
        slot = u % 2
        if kind == "s":
            if stage == 0:
                return [remote(gs.at[1 - c, :, u], r0s.at[slot], s_send.at[u, 0], s_recv.at[u, 0], partner)]
            if stage == 1:
                return [remote(gs.at[c, give[k], u], r1s.at[slot, k], s_send.at[u, 1 + k], s_recv.at[u, 1 + k], n1st)
                        for k in range(2)]
            if stage == 2:
                return [remote(gs.at[c, give2, u], r2s.at[slot], s_send.at[u, 3], s_recv.at[u, 3], n2nd)]
            return [remote(gs.at[c, home, z], r3s.at[i], j_send.at[i], j_recv.at[i], (b % 4 + 4 * z, c))
                    for i, z in enumerate(zpeers)]
        g = ge.at[place(u)]
        if stage == 0:
            return [remote(g.at[1 - c], r0e.at[slot], e_send.at[u, 0], e_recv.at[u, 0], partner)]
        if stage == 1:
            return [remote(g.at[c, give[k]], r1e.at[slot, k], e_send.at[u, 1 + k], e_recv.at[u, 1 + k], n1st)
                    for k in range(2)]
        if stage == 2:
            return [remote(g.at[c, give2], r2e.at[slot], e_send.at[u, 3], e_recv.at[u, 3], n2nd)]
        return [remote(g.at[c, home, z], r3e.at[u, i], e_send.at[u, 4 + i], e_recv.at[u, 4 + i],
                       (b % 4 + 4 * z, c)) for i, z in enumerate(zpeers)]

    def start(kind, u, stage):
        if direct:
            for cp in copies(kind, u, stage):
                cp.start()

    def finish(kind, u, stage):
        for cp in copies(kind, u, stage):
            cp.wait()

    def add_into(dst, src):
        dst[...] = (dst[...].astype(f32) + src[...].astype(f32)).astype(bf16)

    def advance(kind, u, stage):
        finish(kind, u, stage - 1)
        slot = u % 2
        if kind == "s":
            if stage == 1:
                for k in range(4):
                    add_into(gs.at[c, k, u], r0s.at[slot, k])
            elif stage == 2:
                for k in range(2):
                    add_into(gs.at[c, keep[k], u], r1s.at[slot, k])
            elif stage == 3:
                add_into(gs.at[c, home, u], r2s.at[slot])
        else:
            g = ge.at[place(u), c]
            if stage == 1:
                for k in range(4):
                    add_into(g.at[k], r0e.at[slot, k])
            elif stage == 2:
                for k in range(2):
                    add_into(g.at[keep[k]], r1e.at[slot, k])
            elif stage == 3:
                add_into(g.at[home], r2e.at[slot])
        if kind == "e" or stage < 3:
            start(kind, u, stage)

    def settle(kind, u):
        finish(kind, u, 3)
        if kind == "s":
            total = gs[c, home, zz].astype(f32)
            for i in range(nz - 1):
                total = total + r3s[i].astype(f32)
            os_[...] = total
            return
        total = ge[place(u), c, home, zz].astype(f32)
        for i in range(nz - 1):
            total = total + r3e[u, i].astype(f32)
        for h in range(2):
            half = total[24 * h : 24 * h + 24, :]
            if u < 4:
                oe[:, 768 * u + 384 * h : 768 * u + 384 * h + 384] = half
            elif u == 4:
                op[:, 384 * h : 384 * h + 384] = half
            else:
                for w in range(3):
                    at = 768 * w + 256 * (u - 5) + 128 * h
                    oq[:, at : at + 128] = half[:, 128 * w : 128 * w + 128]

    plan = {}
    for j in range(4):
        plan.setdefault(j + 1, []).extend([(1, "s", j), (1, "e", j)])
        plan.setdefault(j + 2, []).extend([(2, "s", j), (2, "e", j)])
        plan.setdefault(j + 3, []).extend([(3, "s", j), (3, "e", j)])
        plan.setdefault(j + 4, []).append((4, "e", j))
    plan.setdefault(7, []).append((5, "s", 0))
    plan.setdefault(9, []).append((6, "s", 0))
    for u, t in ((4, 4), (5, 6), (6, 8), (7, 10)):
        for stage in range(1, 5):
            plan.setdefault(t + stage, []).append((stage, "e", u))

    def tick(t, now=None):
        if not direct:
            return

        def act():
            for stage, kind, u in sorted(plan.get(t, []), key=lambda e: -e[0]):
                if stage == 6 or (stage == 4 and kind == "e"):
                    settle(kind, u)
                elif stage == 5:
                    start("s", 0, 3)
                else:
                    advance(kind, u, stage)

        if plan.get(t):
            if now is None:
                act()
            else:
                pl.when(now == t)(act)

    lane = lane_ids((BLK, 128))
    tiles = ROWS // BLK
    chunk = FF // 4

    def merge(own, other):
        def step(i, _):
            rows = pl.ds(pl.multiple_of(i * BLK, BLK), BLK)
            mine = row_ids((BLK, D)) + i * BLK >= a
            own[rows, :] = jnp.where(mine, own[rows, :].astype(f32), other[rows, :].astype(f32)).astype(bf16)
            return 0
        lax.fori_loop(0, SWAP // BLK, step, 0)

    def turn(src, dst, shift):
        def step(i, _):
            dst[pl.ds(pl.multiple_of(i * BLK, BLK), BLK), :] = rotated(src, shift, i).astype(bf16)
            return 0
        lax.fori_loop(0, tiles, step, 0)

    def expand_shares(slot, i, g):
        half = g.shape[1] // 2
        for n in range(16):
            part = g[24 * n : 24 * n + 24, :]
            part = jnp.concatenate([part[:, 0:half], part[:, half:]], axis=0).astype(bf16)
            yield (slot, n % 2, (n // 2) % 4, 2 * i + n // 8), part

    def front(we, ws, vt):
        loads = [load(src, dst, i) for i, (src, dst) in enumerate(
            ((tok_h, m), (wq_h, wq), (cot_h, n2), (wp_h, wp), (we_h, we), (ws_h, ws)))]
        for cp in loads[:4]:
            cp.start()
        swaps = [
            remote(src.at[pl.ds(0, SWAP)], dst, swap_send.at[i], swap_recv.at[i], partner)
            for i, (src, dst) in enumerate(((tok_h, tok_in), (cot_h, cot_in)))
        ]
        barrier = pltpu.get_barrier_semaphore()
        for f in friends:
            pl.semaphore_signal(barrier, inc=1, device_id=f, device_id_type=MESH)
        pl.semaphore_wait(barrier, len(friends))
        for cp in swaps:
            cp.start()
        for cp in loads[4:]:
            cp.start()
        vec[...] = jnp.zeros_like(vec)
        dn[...] = jnp.zeros_like(dn)
        loads[0].wait()
        swaps[0].wait()
        merge(m, tok_in)
        loads[1].wait()
        bound = jnp.where(c == 0, 0, ROWS - a)

        def project(i, _):
            r = pl.multiple_of(i * BLK, BLK)
            rows = pl.ds(r, BLK)
            xt = rotated(m, a, i)
            x[rows, :] = xt.astype(bf16)
            normed, _unused = row_stats(xt)
            nt_ = (normed * gain1[...].reshape(1, D) + shift1[...].reshape(1, D)).astype(bf16)
            n1[rows, :] = nt_
            qt = nn(nt_, wq[:, 0:D]) + qb[...].reshape(1, D)
            qt = (qt.astype(bf16).astype(f32) * 0.125).astype(bf16)
            q[rows, :] = qt
            qtt = qt.T
            k = nn(nt_, wq[:, D : 2 * D])
            vv = (nn(nt_, wq[:, 2 * D : 3 * D]) + vb[...].reshape(1, D)).astype(bf16)
            v[rows, :] = vv
            vt[:, rows] = vv.T
            k_flag = jnp.where(row_ids((BLK, 128)) + r >= bound, 0.0, masked_score).astype(f32)
            q_flag = jnp.where(lane_ids((1, BLK)) + r >= bound, 1.0, 0.0).astype(f32)
            q_spare = spare_rows(q_flag)
            for p in range(PAIRS):
                kp = k[:, 128 * p : 128 * p + 128]
                for s in range(2):
                    mine = lane < 64 if s == 0 else lane >= 64
                    base = 64 if s == 0 else 0
                    k_aug = jnp.where(lane == base, k_flag, 1.0)
                    k_aug = jnp.where(lane > base + 3, 0.0, k_aug)
                    at = 256 * p + 128 * s
                    kx[rows, at : at + 128] = jnp.where(mine, kp, k_aug).astype(bf16)
                    qxt[at : at + 128, rows] = with_spare(
                        s, qtt[128 * p + 64 * s : 128 * p + 64 * s + 64, :].astype(f32), q_spare)
            return 0

        lax.fori_loop(0, tiles, project, 0)
        triangle = row_ids((BLK, BLK)) <= lane_ids((BLK, BLK))
        jobs = [(i, s) for i in range(tiles) for s in range(2)]

        def attend(p, _):
            at = pl.multiple_of(p * 256, 256)
            pat = pl.multiple_of(p * 128, 128)

            def scores(i, s):
                qt = qxt[pl.ds(at + 128 * s, 128), BLK * i : BLK * i + BLK]
                st = [nn(kx[BLK * k : BLK * k + BLK, pl.ds(at + 128 * s, 128)], qt) for k in range(i + 1)]
                st[i] = jnp.where(triangle, st[i], masked_score)
                return st

            ready = [scores(*job) for job in jobs[:2]]
            for n, (i, s) in enumerate(jobs):
                st = ready.pop(0)
                if n + 2 < len(jobs):
                    ready.append(scores(*jobs[n + 2]))
                cols = slice(BLK * i, BLK * i + BLK)
                peak = jnp.max(st[0], axis=0, keepdims=True)
                for t in st[1:]:
                    peak = jnp.maximum(peak, jnp.max(t, axis=0, keepdims=True))
                vv = jnp.concatenate([vt[pl.ds(pat + 64 * s, 64), :], jnp.ones((16, ROWS), bf16)], axis=0)
                weights = [jnp.exp(t - peak).astype(bf16) for t in st]
                weights = weights[0] if i == 0 else jnp.concatenate(weights, axis=0)
                o = nn(vv[:, 0 : BLK * (i + 1)], weights)
                total = o[64:65, :]
                ctxt[pl.ds(pat + 64 * s, 64), cols] = (o[0:64, :] / total).astype(bf16)
                lse[pl.ds(2 * p + s, 1), cols] = peak + jnp.log(total)
            return 0

        lax.fori_loop(0, PAIRS, attend, 0)
        every = jnp.where(lane_ids((1, ROWS)) >= bound, 1.0, 0.0).astype(f32)
        for h in range(H):
            spare = spare_rows(every, *split3(-lse[h : h + 1, :]))
            at = 128 * h + (64 if h % 2 == 0 else 0)
            qxt[at : at + 64, :] = spare.astype(bf16)
        loads[2].wait()
        swaps[1].wait()
        merge(n2, cot_in)
        turn(n2, cot, a)
        loads[3].wait()

        def add_attended(i, _):
            rows = pl.ds(pl.multiple_of(i * BLK, BLK), BLK)
            mid = tn(ctxt[:, rows], wp[...]) + pb[...].reshape(1, D) + x[rows, :].astype(f32)
            acc[rows, :] = mid
            normed, _unused = row_stats(mid)
            n2[rows, :] = (normed * gain2[...].reshape(1, D) + shift2[...].reshape(1, D)).astype(bf16)
            return 0

        lax.fori_loop(0, tiles, add_attended, 0)
        save = load(acc, mid_h, 6)
        save.start()
        save.wait()
        loads[4].wait()
        loads[5].wait()

    def feed_forward(we, ws, low, grad):
        def one(j, _):
            cols = pl.ds(pl.multiple_of(j * chunk, chunk), chunk)

            def products(t):
                rows = slice(t * BLK, t * BLK + BLK)
                return (nn(n2[rows, :], we[:, cols]) + eb[cols].reshape(1, chunk),
                        nt(cot[rows, :], ws[cols, :]))

            bias_sum = jnp.zeros((1, chunk), f32)
            ready = products(0)
            for t in range(tiles):
                e, da = ready
                if t + 1 < tiles:
                    ready = products(t + 1)
                rows = slice(t * BLK, t * BLK + BLK)
                act, slope = gelu_parts(e)
                act = act.astype(bf16)
                de = (da * slope).astype(bf16)
                low[rows, :] = act
                grad[rows, :] = de
                acc[rows, :] += nn(act, ws[cols, :])
                dn[rows, :] += nt(de, we[:, cols])
                bias_sum = bias_sum + jnp.sum(de.astype(f32), axis=0, keepdims=True)
            vec[pl.ds(8 + j, 1), :] = bias_sum
            for t in range(1, 4):
                tick(t, j)
            for i in range(2):
                g = tn(low[:, 384 * i : 384 * i + 384], cot[...]).astype(bf16)
                for n in range(4):
                    gs[n % 2, 2 * i + n // 2, j] = g[96 * n : 96 * n + 96, :]
            start("s", j, 0)
            for i in range(2):
                for at, part in expand_shares(j, i, tn(n2[:, 384 * i : 384 * i + 384], grad[...])):
                    ge[at] = part
            start("e", j, 0)
            return 0

        lax.fori_loop(0, 4, one, 0)

    def first_half(we, ws):
        pl.run_scoped(functools.partial(front, we, ws), pltpu.VMEM((D, ROWS), bf16))
        pl.run_scoped(functools.partial(feed_forward, we, ws), pltpu.VMEM((ROWS, chunk), bf16), pltpu.VMEM((ROWS, chunk), bf16))

    pl.run_scoped(first_half, pltpu.VMEM((D, FF), bf16), pltpu.VMEM((FF, D), bf16))
    tick(4)

    out_give = [remote(cot.at[pl.ds(0, SWAP)], out_in_h, swap_send.at[2], swap_recv.at[2], partner),
                pltpu.make_async_copy(cot, out_h, out_sem.at[0])]
    ig_give = [remote(n2.at[pl.ds(0, SWAP)], ig_in_h, swap_send.at[3], swap_recv.at[3], partner),
               pltpu.make_async_copy(n2, ig_h, out_sem.at[1])]

    def middle(dot, do):
        def second(mid, ga_all):
            own = load(mid_h, mid, 6)
            own.start()
            own.wait()

            def tile(i, sums):
                r = pl.multiple_of(i * BLK, BLK)
                rows = pl.ds(r, BLK)
                m[rows, :] = (acc[rows, :] + sb[...].reshape(1, D)).astype(bf16)
                back, dgain, dshift = norm_back(mid[rows, :], gain2[...].reshape(1, D), dn[rows, :])
                ct = cot[rows, :].astype(f32)
                dmid = ct + back
                dn[rows, :] = dmid
                ga = dmid.astype(bf16)
                ga_all[rows, :] = ga
                dc = nt(ga, wp[...]).astype(bf16)
                do[rows, :] = dc
                dct = dc.T.astype(f32)
                prod = dct * ctxt[:, rows].astype(f32)
                for h in range(H):
                    inner = jnp.sum(prod[64 * h : 64 * h + 64, :], axis=0, keepdims=True)
                    dot[128 * h : 128 * h + 128, rows] = with_spare(
                        h % 2, dct[64 * h : 64 * h + 64, :], spare_rows(*split3(-inner)))
                dpb = jnp.sum(ga.astype(f32), axis=0, keepdims=True)
                dsb = jnp.sum(ct, axis=0, keepdims=True)
                return tuple(o + n for o, n in zip(sums, (dgain, dshift, dpb, dsb)))

            zero = jnp.zeros((1, D), f32)
            sums = lax.fori_loop(0, tiles, tile, (zero,) * 4)
            for at, s in zip((5, 6, 4, 7), sums):
                vec[at : at + 1, :] = s
            turn(m, cot, ROWS - a)
            for cp in out_give:
                cp.start()
            for i in range(2):
                for at, part in expand_shares(place(4), i, nn(ctxt[384 * i : 384 * i + 384, :], ga_all[...])):
                    ge[at] = part
            start("e", 4, 0)

        pl.run_scoped(second, pltpu.VMEM((ROWS, D), f32), pltpu.VMEM((ROWS, D), bf16))

    def attention(dot, do, dqkv):
        triangle = row_ids((BLK, BLK)) <= lane_ids((BLK, BLK))
        jobs = [(kb, qi, s) for kb in range(tiles) for qi in range(kb, tiles) for s in range(2)]

        def attention_loop(ktr, dqt):
            def pair(p, _):
                at = pl.multiple_of(p * 256, 256)
                pat = pl.multiple_of(p * 128, 128)
                pcols = pl.ds(pat, 128)
                lf = lane_ids((ROWS, 128))
                ktr[...] = jnp.where(lf < 64, kx[:, pl.ds(at, 128)], kx[:, pl.ds(at + 128, 128)]).T

                def scores(kb, qi, s):
                    krows = slice(BLK * kb, BLK * kb + BLK)
                    qrows = slice(BLK * qi, BLK * qi + BLK)
                    head = pl.ds(at + 128 * s, 128)
                    vd = v[krows, pcols]
                    vd = jnp.where(lane < 64 if s == 0 else lane >= 64, vd, jnp.ones_like(vd))
                    return nn(kx[krows, head], qxt[head, qrows]), nn(vd, dot[head, qrows])

                ready = [scores(*job) for job in jobs[:2]]
                dk, dv = {}, {}
                dv_sum = jnp.zeros((1, 128), f32)
                for n, (kb, qi, s) in enumerate(jobs):
                    st, dp = ready.pop(0)
                    if n + 2 < len(jobs):
                        ready.append(scores(*jobs[n + 2]))
                    krows = slice(BLK * kb, BLK * kb + BLK)
                    qrows = slice(BLK * qi, BLK * qi + BLK)
                    prob = jnp.exp(st)
                    if qi == kb:
                        prob = jnp.where(triangle, prob, 0.0)
                    ds = (prob * dp).astype(bf16)
                    dv_part = nn(prob.astype(bf16), do[qrows, pcols])
                    dk_part = nn(ds, q[qrows, pcols])
                    dv[s] = dv_part if qi == kb else dv[s] + dv_part
                    dk[s] = dk_part if qi == kb else dk[s] + dk_part
                    half = slice(64 * s, 64 * s + 64)
                    dq_part = nn(ktr[half, krows], ds)
                    if kb == 0:
                        dqt[half, qrows] = dq_part
                    else:
                        dqt[half, qrows] += dq_part
                    if s == 1 and qi == tiles - 1:
                        dqkv[krows, pl.ds(D + pat, 128)] = jnp.where(lane < 64, dk[0], dk[1]).astype(bf16)
                        dvp = jnp.where(lane < 64, dv[0], dv[1]).astype(bf16)
                        dqkv[krows, pl.ds(2 * D + pat, 128)] = dvp
                        dv_sum = dv_sum + jnp.sum(dvp.astype(f32), axis=0, keepdims=True)
                dq = (dqt[...] * 0.125).astype(bf16).T
                dqkv[:, pcols] = dq
                vec[2:3, pcols] = jnp.sum(dq.astype(f32), axis=0, keepdims=True)
                vec[3:4, pcols] = dv_sum
                for t in range(5, 11):
                    tick(t, p + 5)

                @pl.when(p % 2 == 1)
                def _():
                    k = p // 2
                    for i in range(2):
                        for w in range(3):
                            cols = pl.ds(pl.multiple_of(768 * w + 256 * k, 256), 256)
                            g = tn(n1[:, 384 * i : 384 * i + 384], dqkv[:, cols])
                            for at_, part in expand_shares(place(5 + k), i, g):
                                ge[at_ + (slice(None), slice(128 * w, 128 * w + 128))] = part
                    start("e", 5 + k, 0)

                return 0

            lax.fori_loop(0, PAIRS, pair, 0)

        pl.run_scoped(attention_loop, pltpu.VMEM((128, ROWS), bf16), pltpu.VMEM((128, ROWS), f32))

        def tile(i, sums):
            rows = pl.ds(pl.multiple_of(i * BLK, BLK), BLK)
            g = nt(dqkv[rows, :], wq[...])
            back, dgain, dshift = norm_back(x[rows, :].astype(f32), gain1[...].reshape(1, D), g)
            m[rows, :] = (dn[rows, :] + back).astype(bf16)
            for t in range(11, 15):
                tick(t, i + 11)
            return sums[0] + dgain, sums[1] + dshift

        zero = jnp.zeros((1, D), f32)
        sums = lax.fori_loop(0, tiles, tile, (zero,) * 2)
        vec[0:1, :] = sums[0]
        vec[1:2, :] = sums[1]
        turn(m, n2, ROWS - a)
        for cp in ig_give:
            cp.start()

    def second_half(dot, do):
        middle(dot, do)
        pl.run_scoped(functools.partial(attention, dot, do), pltpu.VMEM((ROWS, 3 * D), bf16))

    pl.run_scoped(second_half, pltpu.VMEM((2 * D, ROWS), bf16), pltpu.VMEM((ROWS, D), bf16))

    ends = list(out_give + ig_give)

    def emit(src, dst):
        cp = pltpu.make_async_copy(src, dst, out_sem.at[len(ends) - 2])
        cp.start()
        ends.append(cp)

    if direct:
        at = 0
        for group in ([partner], [xn], [yn], [(b % 4 + 4 * z, c) for z in zpeers]):
            cps = [remote(vec, vec_in.at[at + i], v_send.at[at + i], v_recv.at[at + i], to)
                   for i, to in enumerate(group)]
            for cp in cps:
                cp.start()
            for cp in cps:
                cp.wait()
            total = vec[...]
            for i in range(len(group)):
                total = total + vec_in[at + i]
            vec[...] = total
            at += len(group)
        emit(vec, vec_h)
        for src, dst in zip((oq, op, oe, os_), grads_h):
            emit(src, dst)
    else:
        emit(vec, vec_h)
        emit(gs, grads_h[0])
        emit(ge, grads_h[1])
    for cp in ends:
        cp.wait()


def layer_call(nz, direct, *args):
    unit = (48, 384)
    if direct:
        grads = [((24, 3 * D), f32), ((24, D), f32), ((24, FF), f32), ((96, D), f32)]
    else:
        grads = [((2, 4, 4, 96, D), bf16), ((8, 2, 4, 4) + unit, bf16)]
    shapes = [((ROWS, D), bf16), ((SWAP, D), bf16), ((ROWS, D), bf16), ((SWAP, D), bf16), ((16, D), f32),
              ((ROWS, D), f32)] + grads
    scratch = [
        pltpu.VMEM((2, 4, 4, 96, D), bf16), pltpu.VMEM((5 if direct else 8, 2, 4, 4) + unit, bf16),
        pltpu.VMEM((SWAP, D), bf16), pltpu.VMEM((SWAP, D), bf16),
        pltpu.VMEM((ROWS, D), bf16), pltpu.VMEM((ROWS, D), bf16),
        pltpu.VMEM((ROWS, D), bf16), pltpu.VMEM((ROWS, D), bf16),
        pltpu.VMEM((ROWS, D), bf16),
        pltpu.VMEM((2 * D, ROWS), bf16), pltpu.VMEM((ROWS, 2 * D), bf16),
        pltpu.VMEM((ROWS, D), bf16), pltpu.VMEM((D, ROWS), bf16),
        pltpu.VMEM((ROWS, D), f32), pltpu.VMEM((ROWS, D), f32),
        pltpu.VMEM((ROWS, D), bf16),
        pltpu.VMEM((D, 3 * D), bf16), pltpu.VMEM((D, D), bf16),
        pltpu.VMEM((16, ROWS), f32),
        pltpu.VMEM((16, D), f32), pltpu.VMEM((6, 16, D), f32),
        pltpu.SemaphoreType.DMA((7,)), pltpu.SemaphoreType.DMA((8,)),
        pltpu.SemaphoreType.DMA((4,)), pltpu.SemaphoreType.DMA((4,)),
    ]
    if direct:
        scratch += [
            pltpu.VMEM((2, 4, 96, D), bf16), pltpu.VMEM((2, 4, nz) + unit, bf16),
            pltpu.VMEM((2, 2, 96, D), bf16), pltpu.VMEM((2, 2, nz) + unit, bf16),
            pltpu.VMEM((2, 96, D), bf16), pltpu.VMEM((2, nz) + unit, bf16),
            pltpu.VMEM((nz - 1, 96, D), bf16), pltpu.VMEM((8, nz - 1) + unit, bf16),
            pltpu.VMEM((24, 3 * D), f32), pltpu.VMEM((24, D), f32), pltpu.VMEM((24, FF), f32), pltpu.VMEM((96, D), f32),
            pltpu.SemaphoreType.DMA((4, 4)), pltpu.SemaphoreType.DMA((4, 4)),
            pltpu.SemaphoreType.DMA((8, 7)), pltpu.SemaphoreType.DMA((8, 7)),
            pltpu.SemaphoreType.DMA((3,)), pltpu.SemaphoreType.DMA((3,)),
            pltpu.SemaphoreType.DMA((6,)), pltpu.SemaphoreType.DMA((6,)),
        ]
    return pl.pallas_call(
        functools.partial(layer_kernel, nz, direct),
        out_shape=[jax.ShapeDtypeStruct(s, t) for s, t in shapes],
        in_specs=[SMEM, ANY, ANY, VMEM, VMEM, ANY, VMEM, VMEM, ANY, VMEM, VMEM, VMEM, ANY, VMEM, ANY, VMEM],
        out_specs=[ANY] * len(shapes),
        scratch_shapes=scratch,
        compiler_params=pltpu.CompilerParams(
            collective_id=0, has_side_effects=True, vmem_limit_bytes=VMEM_LIMIT),
        cost_estimate=pl.CostEstimate(
            flops=64 * 10**9, bytes_accessed=40 * 10**6, transcendentals=20 * 10**6),
        name="layer",
    )(*args)


def swap_back_kernel(lens, out_own, out_in, ig_own, ig_in, out, ig):
    mine = row_ids((BLK, D)) + pl.program_id(0) * BLK >= lens[0, 0]
    out[...] = jnp.where(mine, out_own[...].astype(f32), out_in[...].astype(f32)).astype(bf16)
    ig[...] = jnp.where(mine, ig_own[...].astype(f32), ig_in[...].astype(f32))


def swap_back(lens, out_own, out_in, ig_own, ig_in):
    tile = pl.BlockSpec((BLK, D), lambda i: (i, 0))
    late = pl.BlockSpec((BLK, D), lambda i: (jnp.minimum(i, SWAP // BLK - 1), 0))
    return pl.pallas_call(
        swap_back_kernel,
        grid=(ROWS // BLK,),
        out_shape=[jax.ShapeDtypeStruct((ROWS, D), bf16), jax.ShapeDtypeStruct((ROWS, D), f32)],
        in_specs=[SMEM, tile, late, tile, late],
        out_specs=[tile, tile],
        cost_estimate=pl.CostEstimate(flops=10**6, bytes_accessed=10**7, transcendentals=0),
        name="swap_back",
    )(lens, out_own, out_in, ig_own, ig_in)


def on_device(nz, direct, tokens, lens, gain1, shift1, wq, qb, vb, wp, pb, gain2, shift2, we, eb, ws, sb, cot):
    out_own, out_in, ig_own, ig_in, vec, _mid, *grads = layer_call(
        nz, direct, lens, tokens, cot, gain1, shift1, wq, qb, vb, wp, pb, gain2, shift2, we, eb, ws, sb)
    out, ig = swap_back(lens, out_own, out_in, ig_own, ig_in)
    shards = lax.axis_size("batch") * 2
    me = lax.axis_index("batch") * 2 + lax.axis_index("seq")

    if direct:
        gq, gp, ge, gs = grads

        def own_part(row, rows=1):
            flat = vec[row : row + rows].reshape(rows * D)
            n = rows * D // shards
            return lax.dynamic_slice(flat, (me * n,), (n,))
    else:
        def scatter(g):
            return lax.psum_scatter(g, ("batch", "seq"), scatter_dimension=0, tiled=True)

        def own_part(row, rows=1):
            return scatter(vec[row : row + rows].reshape(rows * D))

        us, ue = (g.astype(f32) for g in grads)
        gs = scatter(us.transpose(2, 1, 0, 3, 4).reshape(FF, D))
        ue = ue.reshape(8, 2, 4, 4, 2, 24, 384)
        wide = ue[:5].transpose(3, 2, 1, 5, 0, 4, 6).reshape(D, 5 * D)
        ge = scatter(wide[:, :FF])
        gp = scatter(wide[:, FF:])
        gq = ue[5:].reshape(3, 2, 4, 4, 2, 24, 3, 128).transpose(3, 2, 1, 5, 6, 0, 4, 7).reshape(D, 3 * D)
        gq = scatter(gq)
    return (out, ig, own_part(0), own_part(1), gq, own_part(2), own_part(3), gp, own_part(4),
            own_part(5), own_part(6), ge, own_part(8, 4), gs, own_part(7))


def solution(mesh):
    nz = mesh.shape["batch"] // 4
    direct = mesh.shape["batch"] == 16 and mesh.shape["seq"] == 2
    rows = P(("batch", "seq"), None)
    part = P(("batch", "seq"))
    whole = P()
    in_specs = (rows, P("batch", None)) + (whole,) * 13 + (rows,)
    out_specs = (rows, rows, part, part, rows, part, part, rows, part, part, part, rows, part, rows, part)
    return jax.shard_map(
        functools.partial(on_device, nz, direct),
        mesh=mesh, in_specs=in_specs, out_specs=out_specs, check_vma=False)
```

```python
import functools
import math

import jax
import jax.numpy as jnp
from jax import lax
from jax.experimental import pallas as pl
from jax.experimental.pallas import tpu as pltpu
from jax.sharding import PartitionSpec as P

f32 = jnp.float32
bf16 = jnp.bfloat16
MESH = pl.DeviceIdType.MESH
ANY = pl.BlockSpec(memory_space=pl.ANY)
VMEM = pl.BlockSpec(memory_space=pltpu.VMEM)
SMEM = pl.BlockSpec(memory_space=pltpu.SMEM)

H = 12
epsilon = 1e-05
masked_score = -1e30
ROWS = 1024
SWAP = 768
D = 768
FF = 3072
PAIRS = 6
BLK = 256
VMEM_LIMIT = 65000 * 2**10
GELU_C = 0.7978845608028654


def nn(a, b):
    return lax.dot_general(a, b, (((1,), (0,)), ((), ())), preferred_element_type=f32)


def nt(a, b):
    return lax.dot_general(a, b, (((1,), (1,)), ((), ())), preferred_element_type=f32)


def tn(a, b):
    return lax.dot_general(a, b, (((0,), (0,)), ((), ())), preferred_element_type=f32)


def row_stats(v):
    mean = jnp.mean(v, axis=-1, keepdims=True)
    centered = v - mean
    var = jnp.mean(centered * centered, axis=-1, keepdims=True)
    return centered * lax.rsqrt(var + epsilon), lax.rsqrt(var + epsilon)


def lane_ids(shape):
    return lax.broadcasted_iota(jnp.int32, shape, 1)


def row_ids(shape):
    return lax.broadcasted_iota(jnp.int32, shape, 0)


def split3(v):
    hi = v.astype(bf16).astype(f32)
    rest = v - hi
    mid = rest.astype(bf16).astype(f32)
    return hi, mid, rest - mid


def rotated(m, shift, i):
    coarse = lax.shift_right_logical(shift, 8)
    fine = lax.bitwise_and(shift, 255)

    def two(k):
        blocks = [m[pl.ds(pl.multiple_of(((i + k + n) % 4) * BLK, BLK), BLK), :] for n in range(2)]
        return jnp.concatenate(blocks, axis=0)

    part = jnp.where(coarse == 1, two(1), jnp.where(coarse == 2, two(2), two(3)))
    shape = (BLK, 2 * BLK)
    pick = (lane_ids(shape) == row_ids(shape) + fine).astype(f32).astype(bf16)
    return nn(pick, part)


def norm_back(v, gain, r):
    n, scale = row_stats(v)
    u = gain * r
    back = scale * (u - jnp.mean(u, axis=-1, keepdims=True) - n * jnp.mean(u * n, axis=-1, keepdims=True))
    return back, jnp.sum(r * n, axis=0, keepdims=True), jnp.sum(r, axis=0, keepdims=True)


def gelu_parts(e):
    sq = e * e
    th = jnp.tanh(e * (GELU_C + (GELU_C * 0.044715) * sq))
    half = 0.5 + 0.5 * th
    slope = half + (e * (1.0 - th * th)) * (0.5 * GELU_C + (1.5 * GELU_C * 0.044715) * sq)
    return e * half, slope


def spare_rows(*rows):
    ids = row_ids((64, rows[0].shape[1]))
    out = jnp.zeros(ids.shape, f32)
    for i, row in enumerate(rows):
        out = jnp.where(ids == i, row, out)
    return out


def with_spare(s, part, spare):
    return jnp.concatenate([part, spare] if s == 0 else [spare, part], axis=0).astype(bf16)


def layer_kernel(
    nz, direct,
    lens, tok_h, cot_h, gain1, shift1, wq_h, qb, vb, wp_h, pb, gain2, shift2, we_h, eb, ws_h, sb,
    *rest,
):
    n_out = 10 if direct else 8
    out_h, out_in_h, ig_h, ig_in_h, vec_h, mid_h = rest[:6]
    grads_h = rest[6:n_out]
    (gs, ge, tok_in, cot_in, m, cot, x, n1, q, qxt, kx, v, ctxt, acc, dn, n2, wq, wp, lse, vec, vec_in,
     load_sem, out_sem, swap_send, swap_recv) = rest[n_out : n_out + 25]
    if direct:
        (r0s, r0e, r1s, r1e, r2s, r2e, r3s, r3e, oq, op, oe, os_,
         s_send, s_recv, e_send, e_recv, j_send, j_recv, v_send, v_recv) = rest[n_out + 25 :]
    b = lax.axis_index("batch")
    c = lax.axis_index("seq")
    a = lens[0, 0]
    xx = b % 2
    yy = (b // 2) % 2
    zz = b // 4
    partner = (b, 1 - c)
    n1st = (b + (1 - c) * (1 - 2 * xx) + c * (2 - 4 * yy), c)
    n2nd = (b + c * (1 - 2 * xx) + (1 - c) * (2 - 4 * yy), c)
    zpeers = [(zz + i) % nz for i in range(1, nz)] if direct else []
    keep = [(1 - c) * (2 * k + xx) + c * (2 * yy + k) for k in range(2)]
    give = [(1 - c) * (2 * k + 1 - xx) + c * (2 * (1 - yy) + k) for k in range(2)]
    give2 = (1 - c) * (2 * (1 - yy) + xx) + c * (2 * yy + 1 - xx)
    home = 2 * yy + xx
    friends = [partner]
    if direct:
        cube = [(b - b % 4 + (yy + n // 2) % 2 * 2 + (xx + n) % 2, (c + n // 4) % 2) for n in range(1, 8)]
        friends = cube + [(b % 4 + 4 * z, c) for z in zpeers]

    def load(src, dst, i):
        return pltpu.make_async_copy(src, dst, load_sem.at[i])

    def remote(src, dst, send, recv, to):
        return pltpu.make_async_remote_copy(
            src_ref=src, dst_ref=dst, send_sem=send, recv_sem=recv,
            device_id=to, device_id_type=MESH)

    def place(u):
        return u if not direct else u % 5

    def copies(kind, u, stage):
        slot = u % 2
        if kind == "s":
            if stage == 0:
                return [remote(gs.at[1 - c, :, u], r0s.at[slot], s_send.at[u, 0], s_recv.at[u, 0], partner)]
            if stage == 1:
                return [remote(gs.at[c, give[k], u], r1s.at[u % 4, k], s_send.at[u, 1 + k], s_recv.at[u, 1 + k], n1st)
                        for k in range(2)]
            if stage == 2:
                return [remote(gs.at[c, give2, u], r2s.at[u % 4], s_send.at[u, 3], s_recv.at[u, 3], n2nd)]
            return [remote(gs.at[c, home, z], r3s.at[i], j_send.at[i], j_recv.at[i], (b % 4 + 4 * z, c))
                    for i, z in enumerate(zpeers)]
        g = ge.at[place(u)]
        if stage == 0:
            return [remote(g.at[1 - c], r0e.at[slot], e_send.at[u, 0], e_recv.at[u, 0], partner)]
        if stage == 1:
            return [remote(g.at[c, give[k]], r1e.at[u % 4, k], e_send.at[u, 1 + k], e_recv.at[u, 1 + k], n1st)
                    for k in range(2)]
        if stage == 2:
            return [remote(g.at[c, give2], r2e.at[u % 4], e_send.at[u, 3], e_recv.at[u, 3], n2nd)]
        return [remote(g.at[c, home, z], r3e.at[u % 4, i], e_send.at[u, 4 + i], e_recv.at[u, 4 + i],
                       (b % 4 + 4 * z, c)) for i, z in enumerate(zpeers)]

    def start(kind, u, stage):
        if direct:
            for cp in copies(kind, u, stage):
                cp.start()

    def finish(kind, u, stage):
        for cp in copies(kind, u, stage):
            cp.wait()

    def add_into(dst, src):
        dst[...] = dst[...] + src[...]

    def advance(kind, u, stage):
        finish(kind, u, stage - 1)
        slot = u % 2
        if kind == "s":
            if stage == 1:
                for k in range(4):
                    add_into(gs.at[c, k, u], r0s.at[slot, k])
            elif stage == 2:
                for k in range(2):
                    add_into(gs.at[c, keep[k], u], r1s.at[u % 4, k])
            elif stage == 3:
                add_into(gs.at[c, home, u], r2s.at[u % 4])
        else:
            g = ge.at[place(u), c]
            if stage == 1:
                for k in range(4):
                    add_into(g.at[k], r0e.at[slot, k])
            elif stage == 2:
                for k in range(2):
                    add_into(g.at[keep[k]], r1e.at[u % 4, k])
            elif stage == 3:
                add_into(g.at[home], r2e.at[u % 4])
        if kind == "e" or stage < 3:
            start(kind, u, stage)

    def settle(kind, u):
        finish(kind, u, 3)
        if kind == "s":
            total = gs[c, home, zz].astype(f32)
            for i in range(nz - 1):
                total = total + r3s[i].astype(f32)
            os_[...] = total
            return
        total = ge[place(u), c, home, zz].astype(f32)
        for i in range(nz - 1):
            total = total + r3e[u % 4, i].astype(f32)
        for h in range(2):
            half = total[24 * h : 24 * h + 24, :]
            if u < 4:
                oe[:, 768 * u + 384 * h : 768 * u + 384 * h + 384] = half
            elif u == 4:
                op[:, 384 * h : 384 * h + 384] = half
            else:
                for w in range(3):
                    at = 768 * w + 256 * (u - 5) + 128 * h
                    oq[:, at : at + 128] = half[:, 128 * w : 128 * w + 128]

    def steps(todo, when=None):
        if not direct:
            return

        def act():
            for kind, u, stage in todo:
                if stage == 4:
                    settle(kind, u)
                elif stage == "join":
                    start(kind, u, 3)
                else:
                    advance(kind, u, stage)

        if when is None:
            act()
        else:
            pl.when(when)(act)

    lane = lane_ids((BLK, 128))
    tiles = ROWS // BLK
    chunk = FF // 4

    def merge(own, other):
        def step(i, _):
            rows = pl.ds(pl.multiple_of(i * BLK, BLK), BLK)
            mine = row_ids((BLK, D)) + i * BLK >= a
            own[rows, :] = jnp.where(mine, own[rows, :].astype(f32), other[rows, :].astype(f32)).astype(bf16)
            return 0
        lax.fori_loop(0, SWAP // BLK, step, 0)

    def turn(src, dst, shift):
        def step(i, _):
            dst[pl.ds(pl.multiple_of(i * BLK, BLK), BLK), :] = rotated(src, shift, i).astype(bf16)
            return 0
        lax.fori_loop(0, tiles, step, 0)

    def expand_shares(slot, i, g):
        half = g.shape[1] // 2
        for n in range(16):
            part = g[24 * n : 24 * n + 24, :]
            part = jnp.concatenate([part[:, 0:half], part[:, half:]], axis=0).astype(bf16)
            yield (slot, n % 2, (n // 2) % 4, 2 * i + n // 8), part

    def front(we, ws, vt):
        loads = [load(src, dst, i) for i, (src, dst) in enumerate(
            ((tok_h, m), (wq_h, wq), (cot_h, n2), (wp_h, wp), (we_h, we), (ws_h, ws)))]
        for cp in loads[:4]:
            cp.start()
        swaps = [
            remote(src.at[pl.ds(0, SWAP)], dst, swap_send.at[i], swap_recv.at[i], partner)
            for i, (src, dst) in enumerate(((tok_h, tok_in), (cot_h, cot_in)))
        ]
        barrier = pltpu.get_barrier_semaphore()
        for f in friends:
            pl.semaphore_signal(barrier, inc=1, device_id=f, device_id_type=MESH)
        pl.semaphore_wait(barrier, len(friends))
        for cp in swaps:
            cp.start()
        for cp in loads[4:]:
            cp.start()
        vec[...] = jnp.zeros_like(vec)
        dn[...] = jnp.zeros_like(dn)
        loads[0].wait()
        swaps[0].wait()
        merge(m, tok_in)
        loads[1].wait()
        bound = jnp.where(c == 0, 0, ROWS - a)

        def project(i, _):
            r = pl.multiple_of(i * BLK, BLK)
            rows = pl.ds(r, BLK)
            xt = rotated(m, a, i)
            x[rows, :] = xt.astype(bf16)
            normed, _unused = row_stats(xt)
            nt_ = (normed * gain1[...].reshape(1, D) + shift1[...].reshape(1, D)).astype(bf16)
            n1[rows, :] = nt_
            qt = nn(nt_, wq[:, 0:D]) + qb[...].reshape(1, D)
            qt = (qt.astype(bf16).astype(f32) * 0.125).astype(bf16)
            q[rows, :] = qt
            qtt = qt.T
            k = nn(nt_, wq[:, D : 2 * D])
            vv = (nn(nt_, wq[:, 2 * D : 3 * D]) + vb[...].reshape(1, D)).astype(bf16)
            v[rows, :] = vv
            vt[:, rows] = vv.T
            k_flag = jnp.where(row_ids((BLK, 128)) + r >= bound, 0.0, masked_score).astype(f32)
            q_flag = jnp.where(lane_ids((1, BLK)) + r >= bound, 1.0, 0.0).astype(f32)
            q_spare = spare_rows(q_flag)
            for p in range(PAIRS):
                kp = k[:, 128 * p : 128 * p + 128]
                for s in range(2):
                    mine = lane < 64 if s == 0 else lane >= 64
                    base = 64 if s == 0 else 0
                    k_aug = jnp.where(lane == base, k_flag, 1.0)
                    k_aug = jnp.where(lane > base + 3, 0.0, k_aug)
                    at = 256 * p + 128 * s
                    kx[rows, at : at + 128] = jnp.where(mine, kp, k_aug).astype(bf16)
                    qxt[at : at + 128, rows] = with_spare(
                        s, qtt[128 * p + 64 * s : 128 * p + 64 * s + 64, :].astype(f32), q_spare)
            return 0

        lax.fori_loop(0, tiles, project, 0)
        triangle = row_ids((BLK, BLK)) <= lane_ids((BLK, BLK))
        jobs = [(i, s) for i in range(tiles) for s in range(2)]

        def attend(p, _):
            at = pl.multiple_of(p * 256, 256)
            pat = pl.multiple_of(p * 128, 128)

            def scores(i, s):
                qt = qxt[pl.ds(at + 128 * s, 128), BLK * i : BLK * i + BLK]
                st = [nn(kx[BLK * k : BLK * k + BLK, pl.ds(at + 128 * s, 128)], qt) for k in range(i + 1)]
                st[i] = jnp.where(triangle, st[i], masked_score)
                return st

            ready = [scores(*job) for job in jobs[:2]]
            for n, (i, s) in enumerate(jobs):
                st = ready.pop(0)
                if n + 2 < len(jobs):
                    ready.append(scores(*jobs[n + 2]))
                cols = slice(BLK * i, BLK * i + BLK)
                peak = jnp.max(st[0], axis=0, keepdims=True)
                for t in st[1:]:
                    peak = jnp.maximum(peak, jnp.max(t, axis=0, keepdims=True))
                vv = jnp.concatenate([vt[pl.ds(pat + 64 * s, 64), :], jnp.ones((16, ROWS), bf16)], axis=0)
                weights = [jnp.exp(t - peak).astype(bf16) for t in st]
                weights = weights[0] if i == 0 else jnp.concatenate(weights, axis=0)
                o = nn(vv[:, 0 : BLK * (i + 1)], weights)
                total = o[64:65, :]
                ctxt[pl.ds(pat + 64 * s, 64), cols] = (o[0:64, :] / total).astype(bf16)
                lse[pl.ds(2 * p + s, 1), cols] = peak + jnp.log(total)
            return 0

        lax.fori_loop(0, PAIRS, attend, 0)
        every = jnp.where(lane_ids((1, ROWS)) >= bound, 1.0, 0.0).astype(f32)
        for h in range(H):
            spare = spare_rows(every, *split3(-lse[h : h + 1, :]))
            at = 128 * h + (64 if h % 2 == 0 else 0)
            qxt[at : at + 64, :] = spare.astype(bf16)
        loads[2].wait()
        swaps[1].wait()
        merge(n2, cot_in)
        turn(n2, cot, a)
        loads[3].wait()

        def add_attended(i, _):
            rows = pl.ds(pl.multiple_of(i * BLK, BLK), BLK)
            mid = tn(ctxt[:, rows], wp[...]) + pb[...].reshape(1, D) + x[rows, :].astype(f32)
            acc[rows, :] = mid
            normed, _unused = row_stats(mid)
            n2[rows, :] = (normed * gain2[...].reshape(1, D) + shift2[...].reshape(1, D)).astype(bf16)
            pltpu.make_async_copy(acc.at[rows], mid_h.at[rows], load_sem.at[6]).start()
            return 0

        lax.fori_loop(0, tiles, add_attended, 0)
        load(acc, mid_h, 6).wait()
        loads[4].wait()
        loads[5].wait()

    def feed_forward(we, ws, grad):
        low = m

        def one(j, _):
            cols = pl.ds(pl.multiple_of(j * chunk, chunk), chunk)

            def products(t):
                rows = slice(t * BLK, t * BLK + BLK)
                return (nn(n2[rows, :], we[:, cols]) + eb[cols].reshape(1, chunk),
                        nt(cot[rows, :], ws[cols, :]))

            bias_sum = jnp.zeros((1, chunk), f32)
            ready = products(0)
            for t in range(tiles):
                e, da = ready
                if t + 1 < tiles:
                    ready = products(t + 1)
                rows = slice(t * BLK, t * BLK + BLK)
                act, slope = gelu_parts(e)
                act = act.astype(bf16)
                de = (da * slope).astype(bf16)
                low[rows, :] = act
                grad[rows, :] = de
                acc[rows, :] += nn(act, ws[cols, :])
                dn[rows, :] += nt(de, we[:, cols])
                bias_sum = bias_sum + jnp.sum(de.astype(f32), axis=0, keepdims=True)
                if t == 0:
                    steps([("s", j - 2, 2)], j >= 2)
                elif t == 1:
                    steps([("s", j - 1, 1)], j >= 1)
                elif t == 2:
                    steps([("e", j - 3, 2)], j >= 3)
                else:
                    steps([("e", j - 1, 1)], j >= 1)
            vec[pl.ds(8 + j, 1), :] = bias_sum
            for i in range(2):
                g = tn(low[:, 384 * i : 384 * i + 384], cot[...]).astype(bf16)
                for n in range(4):
                    gs[n % 2, 2 * i + n // 2, j] = g[96 * n : 96 * n + 96, :]
            start("s", j, 0)
            for i in range(2):
                for at, part in expand_shares(j, i, tn(n2[:, 384 * i : 384 * i + 384], grad[...])):
                    ge[at] = part
            start("e", j, 0)
            return 0

        lax.fori_loop(0, 4, one, 0)

    def first_half(we, ws):
        pl.run_scoped(functools.partial(front, we, ws), pltpu.VMEM((D, ROWS), bf16))
        pl.run_scoped(functools.partial(feed_forward, we, ws), pltpu.VMEM((ROWS, chunk), bf16))

    pl.run_scoped(first_half, pltpu.VMEM((D, FF), bf16), pltpu.VMEM((FF, D), bf16))
    def total_copies(n):
        to = cube if n == 0 else [(b % 4 + 4 * z, c) for z in zpeers]
        at = 7 * n
        return [remote(vec, vec_in.at[at + i], v_send.at[at + i], v_recv.at[at + i], t) for i, t in enumerate(to)]

    def total_hop(n):
        for cp in total_copies(n):
            cp.wait()
        total = vec[...]
        for i in range(len(total_copies(n))):
            total = total + vec_in[7 * n + i]
        vec[...] = total

    out_give = [remote(cot.at[pl.ds(0, SWAP)], out_in_h, swap_send.at[2], swap_recv.at[2], partner),
                pltpu.make_async_copy(cot, out_h, out_sem.at[0])]
    ig_give = [remote(n2.at[pl.ds(0, SWAP)], ig_in_h, swap_send.at[3], swap_recv.at[3], partner),
               pltpu.make_async_copy(n2, ig_h, out_sem.at[1])]

    def middle(dot, do):
        def second(mid, ga_all):
            own = load(mid_h, mid, 6)
            own.start()
            own.wait()

            def tile(i, sums):
                rows = slice(i * BLK, i * BLK + BLK)
                m[rows, :] = (acc[rows, :] + sb[...].reshape(1, D)).astype(bf16)
                back, dgain, dshift = norm_back(mid[rows, :], gain2[...].reshape(1, D), dn[rows, :])
                ct = cot[rows, :].astype(f32)
                dmid = ct + back
                dn[rows, :] = dmid
                ga = dmid.astype(bf16)
                ga_all[rows, :] = ga
                dc = nt(ga, wp[...]).astype(bf16)
                do[rows, :] = dc
                dct = dc.T.astype(f32)
                prod = dct * ctxt[:, rows].astype(f32)
                for h in range(H):
                    inner = jnp.sum(prod[64 * h : 64 * h + 64, :], axis=0, keepdims=True)
                    dot[128 * h : 128 * h + 128, rows] = with_spare(
                        h % 2, dct[64 * h : 64 * h + 64, :], spare_rows(*split3(-inner)))
                for n, todo in enumerate((
                    [("s", 3, 1)], [("e", 3, 1)], [("e", 1, 2)], [("s", 2, 2)])):
                    if i == n:
                        steps(todo)
                dpb = jnp.sum(ga.astype(f32), axis=0, keepdims=True)
                dsb = jnp.sum(ct, axis=0, keepdims=True)
                return tuple(o + n for o, n in zip(sums, (dgain, dshift, dpb, dsb)))

            zero = jnp.zeros((1, D), f32)
            sums = (zero,) * 4
            for i in range(tiles):
                sums = tile(i, sums)
            for at, s in zip((5, 6, 4, 7), sums):
                vec[at : at + 1, :] = s
            turn(m, cot, ROWS - a)
            for cp in out_give:
                cp.start()
            for i in range(2):
                for at, part in expand_shares(place(4), i, nn(ctxt[384 * i : 384 * i + 384, :], ga_all[...])):
                    ge[at] = part
            start("e", 4, 0)

        pl.run_scoped(second, pltpu.VMEM((ROWS, D), f32), pltpu.VMEM((ROWS, D), bf16))

    def attention(dot, do, dqkv):
        triangle = row_ids((BLK, BLK)) <= lane_ids((BLK, BLK))
        jobs = [(kb, qi, s) for kb in range(tiles) for qi in range(kb, tiles) for s in range(2)]

        def attention_loop(ktr, dqt):
            def pair(p, _):
                at = pl.multiple_of(p * 256, 256)
                pat = pl.multiple_of(p * 128, 128)
                pcols = pl.ds(pat, 128)
                lf = lane_ids((ROWS, 128))
                ktr[...] = jnp.where(lf < 64, kx[:, pl.ds(at, 128)], kx[:, pl.ds(at + 128, 128)]).T

                def scores(kb, qi, s):
                    krows = slice(BLK * kb, BLK * kb + BLK)
                    qrows = slice(BLK * qi, BLK * qi + BLK)
                    head = pl.ds(at + 128 * s, 128)
                    vd = v[krows, pcols]
                    vd = jnp.where(lane < 64 if s == 0 else lane >= 64, vd, jnp.ones_like(vd))
                    return nn(kx[krows, head], qxt[head, qrows]), nn(vd, dot[head, qrows])

                ready = [scores(*job) for job in jobs[:2]]
                dk, dv = {}, {}
                dv_sum = jnp.zeros((1, 128), f32)
                for n, (kb, qi, s) in enumerate(jobs):
                    st, dp = ready.pop(0)
                    if n + 2 < len(jobs):
                        ready.append(scores(*jobs[n + 2]))
                    krows = slice(BLK * kb, BLK * kb + BLK)
                    qrows = slice(BLK * qi, BLK * qi + BLK)
                    prob = jnp.exp(st)
                    if qi == kb:
                        prob = jnp.where(triangle, prob, 0.0)
                    ds = (prob * dp).astype(bf16)
                    dv_part = nn(prob.astype(bf16), do[qrows, pcols])
                    dk_part = nn(ds, q[qrows, pcols])
                    dv[s] = dv_part if qi == kb else dv[s] + dv_part
                    dk[s] = dk_part if qi == kb else dk[s] + dk_part
                    half = slice(64 * s, 64 * s + 64)
                    dq_part = nn(ktr[half, krows], ds)
                    if kb == 0:
                        dqt[half, qrows] = dq_part
                    else:
                        dqt[half, qrows] += dq_part
                    if n == len(jobs) // 2:
                        for r, todo in enumerate((
                            [("s", 0, 3), ("e", 0, 3), ("s", 1, 3), ("e", 2, 2), ("e", 4, 1)],
                            [("e", 0, 4), ("e", 1, 3), ("s", 3, 2), ("e", 3, 2)],
                            [("s", 2, 3), ("e", 2, 3), ("e", 4, 2), ("e", 5, 1)],
                            [("e", 1, 4), ("s", 3, 3), ("e", 3, 3)],
                            [("e", 2, 4), ("s", 0, "join"), ("e", 4, 3), ("e", 5, 2), ("e", 6, 1)],
                            [("e", 3, 4)])):
                            steps(todo, p == r)
                    if s == 1 and qi == tiles - 1:
                        dqkv[krows, pl.ds(D + pat, 128)] = jnp.where(lane < 64, dk[0], dk[1]).astype(bf16)
                        dvp = jnp.where(lane < 64, dv[0], dv[1]).astype(bf16)
                        dqkv[krows, pl.ds(2 * D + pat, 128)] = dvp
                        dv_sum = dv_sum + jnp.sum(dvp.astype(f32), axis=0, keepdims=True)
                dq = (dqt[...] * 0.125).astype(bf16).T
                dqkv[:, pcols] = dq
                vec[2:3, pcols] = jnp.sum(dq.astype(f32), axis=0, keepdims=True)
                vec[3:4, pcols] = dv_sum
                @pl.when(p % 2 == 1)
                def _():
                    k = p // 2
                    for i in range(2):
                        for w in range(3):
                            cols = pl.ds(pl.multiple_of(768 * w + 256 * k, 256), 256)
                            g = tn(n1[:, 384 * i : 384 * i + 384], dqkv[:, cols])
                            for at_, part in expand_shares(place(5 + k), i, g):
                                ge[at_ + (slice(None), slice(128 * w, 128 * w + 128))] = part
                    start("e", 5 + k, 0)

                return 0

            lax.fori_loop(0, PAIRS, pair, 0)

        pl.run_scoped(attention_loop, pltpu.VMEM((128, ROWS), bf16), pltpu.VMEM((128, ROWS), f32))

        def tile(i, sums):
            rows = pl.ds(pl.multiple_of(i * BLK, BLK), BLK)
            g = nt(dqkv[rows, :], wq[...])
            back, dgain, dshift = norm_back(x[rows, :].astype(f32), gain1[...].reshape(1, D), g)
            m[rows, :] = (dn[rows, :] + back).astype(bf16)
            for n, todo in enumerate((
                [("e", 4, 4), ("e", 5, 3), ("e", 6, 2), ("e", 7, 1)], [("s", 0, 4)], [], [("e", 7, 2)])):
                steps(todo, i == n)
            return sums[0] + dgain, sums[1] + dshift

        zero = jnp.zeros((1, D), f32)
        sums = lax.fori_loop(0, tiles, tile, (zero,) * 2)
        vec[0:1, :] = sums[0]
        vec[1:2, :] = sums[1]
        if direct:
            for cp in total_copies(0):
                cp.start()
        turn(m, n2, ROWS - a)
        for cp in ig_give:
            cp.start()

    def second_half(dot, do):
        middle(dot, do)
        pl.run_scoped(functools.partial(attention, dot, do), pltpu.VMEM((ROWS, 3 * D), bf16))

    pl.run_scoped(second_half, pltpu.VMEM((2 * D, ROWS), bf16), pltpu.VMEM((ROWS, D), bf16))

    ends = list(out_give + ig_give)

    def emit(src, dst):
        cp = pltpu.make_async_copy(src, dst, out_sem.at[len(ends) - 2])
        cp.start()
        ends.append(cp)

    if direct:
        steps([("e", 5, 4), ("e", 6, 3), ("e", 7, 3)])
        total_hop(0)
        for cp in total_copies(1):
            cp.start()
        steps([("e", 6, 4), ("e", 7, 4)])
        total_hop(1)
        emit(vec, vec_h)
        for src, dst in zip((oq, op, oe, os_), grads_h):
            emit(src, dst)
    else:
        emit(vec, vec_h)
        emit(gs, grads_h[0])
        emit(ge, grads_h[1])
    for cp in ends:
        cp.wait()


def layer_call(nz, direct, *args):
    unit = (48, 384)
    if direct:
        grads = [((24, 3 * D), f32), ((24, D), f32), ((24, FF), f32), ((96, D), f32)]
    else:
        grads = [((2, 4, 4, 96, D), bf16), ((8, 2, 4, 4) + unit, bf16)]
    shapes = [((ROWS, D), bf16), ((SWAP, D), bf16), ((ROWS, D), bf16), ((SWAP, D), bf16), ((16, D), f32),
              ((ROWS, D), f32)] + grads
    scratch = [
        pltpu.VMEM((2, 4, 4, 96, D), bf16), pltpu.VMEM((5 if direct else 8, 2, 4, 4) + unit, bf16),
        pltpu.VMEM((SWAP, D), bf16), pltpu.VMEM((SWAP, D), bf16),
        pltpu.VMEM((ROWS, D), bf16), pltpu.VMEM((ROWS, D), bf16),
        pltpu.VMEM((ROWS, D), bf16), pltpu.VMEM((ROWS, D), bf16),
        pltpu.VMEM((ROWS, D), bf16),
        pltpu.VMEM((2 * D, ROWS), bf16), pltpu.VMEM((ROWS, 2 * D), bf16),
        pltpu.VMEM((ROWS, D), bf16), pltpu.VMEM((D, ROWS), bf16),
        pltpu.VMEM((ROWS, D), f32), pltpu.VMEM((ROWS, D), f32),
        pltpu.VMEM((ROWS, D), bf16),
        pltpu.VMEM((D, 3 * D), bf16), pltpu.VMEM((D, D), bf16),
        pltpu.VMEM((16, ROWS), f32),
        pltpu.VMEM((16, D), f32), pltpu.VMEM((10 if direct else 1, 16, D), f32),
        pltpu.SemaphoreType.DMA((7,)), pltpu.SemaphoreType.DMA((8,)),
        pltpu.SemaphoreType.DMA((4,)), pltpu.SemaphoreType.DMA((4,)),
    ]
    if direct:
        scratch += [
            pltpu.VMEM((2, 4, 96, D), bf16), pltpu.VMEM((2, 4, nz) + unit, bf16),
            pltpu.VMEM((4, 2, 96, D), bf16), pltpu.VMEM((4, 2, nz) + unit, bf16),
            pltpu.VMEM((4, 96, D), bf16), pltpu.VMEM((4, nz) + unit, bf16),
            pltpu.VMEM((nz - 1, 96, D), bf16), pltpu.VMEM((4, nz - 1) + unit, bf16),
            pltpu.VMEM((24, 3 * D), f32), pltpu.VMEM((24, D), f32), pltpu.VMEM((24, FF), f32), pltpu.VMEM((96, D), f32),
            pltpu.SemaphoreType.DMA((4, 4)), pltpu.SemaphoreType.DMA((4, 4)),
            pltpu.SemaphoreType.DMA((8, 7)), pltpu.SemaphoreType.DMA((8, 7)),
            pltpu.SemaphoreType.DMA((3,)), pltpu.SemaphoreType.DMA((3,)),
            pltpu.SemaphoreType.DMA((10,)), pltpu.SemaphoreType.DMA((10,)),
        ]
    return pl.pallas_call(
        functools.partial(layer_kernel, nz, direct),
        out_shape=[jax.ShapeDtypeStruct(s, t) for s, t in shapes],
        in_specs=[SMEM, ANY, ANY, VMEM, VMEM, ANY, VMEM, VMEM, ANY, VMEM, VMEM, VMEM, ANY, VMEM, ANY, VMEM],
        out_specs=[ANY] * len(shapes),
        scratch_shapes=scratch,
        compiler_params=pltpu.CompilerParams(
            collective_id=0, has_side_effects=True, vmem_limit_bytes=VMEM_LIMIT),
        cost_estimate=pl.CostEstimate(
            flops=64 * 10**9, bytes_accessed=40 * 10**6, transcendentals=20 * 10**6),
        name="layer",
    )(*args)


def final_kernel(
    direct, shards, lens, out_own, out_in, ig_own, ig_in, vec, *rest,
):
    moved = 4 if direct else 0
    given = 9 if direct else 0
    grads = rest[:moved]
    out, ig = rest[moved : moved + 2]
    grads_to = rest[moved + 2 : 2 * moved + 2]
    parts = rest[2 * moved + 2 : 2 * moved + 2 + given]
    own, inn, igo, igi, res, load_sem, save_sem = rest[2 * moved + 2 + given :]
    a = lens[0, 0]
    tiles = ROWS // BLK
    loads = []
    for t in range(tiles):
        rows = pl.ds(t * BLK, BLK)
        some = [(ig_own, igo), (out_own, own)]
        if t * BLK < SWAP:
            some += [(ig_in, igi), (out_in, inn)]
        loads.append([pltpu.make_async_copy(src.at[rows], dst.at[rows], load_sem.at[t, i])
                      for i, (src, dst) in enumerate(some)])
    for group in loads:
        for cp in group:
            cp.start()
    for src, dst in zip(grads, grads_to):
        dst[...] = src[...]
    if direct:
        me = lax.axis_index("batch") * 2 + lax.axis_index("seq")

        def columns(v, first, n):
            shape = (D, 128)
            pick = (row_ids(shape) == lane_ids(shape) + first) & (lane_ids(shape) < n)
            return jnp.dot(v, pick.astype(f32), precision=lax.Precision.HIGHEST, preferred_element_type=f32)

        n = D // shards
        narrow = columns(vec[...], n * me, n)
        for i in range(8):
            parts[i][...] = narrow[i, :n]
        n = FF // shards
        wide = columns(vec[8:12, :], n * (me % (D // n)), n)
        wide = jnp.sum(jnp.where(row_ids(wide.shape) == me // (D // n), wide, 0.0), axis=0)
        parts[8][...] = wide[:n]
    saves = []
    for t in range(tiles):
        for cp in loads[t]:
            cp.wait()
        rows = slice(t * BLK, t * BLK + BLK)
        g = igo[rows, :].astype(f32)
        if t * BLK < SWAP:
            mine = row_ids((BLK, D)) + t * BLK >= a
            own[rows, :] = jnp.where(mine, own[rows, :].astype(f32), inn[rows, :].astype(f32)).astype(bf16)
            g = jnp.where(mine, g, igi[rows, :].astype(f32))
        res[rows, :] = g
        for i, (src, dst) in enumerate(((own, out), (res, ig))):
            saves.append(pltpu.make_async_copy(src.at[pl.ds(t * BLK, BLK)], dst.at[pl.ds(t * BLK, BLK)], save_sem.at[t, i]))
            saves[-1].start()
    for cp in saves:
        cp.wait()


def final_call(direct, shards, lens, out_own, out_in, ig_own, ig_in, vec, *grads):
    tiles = ROWS // BLK
    parts = [D // shards] * 8 + [FF // shards] if direct else []
    return pl.pallas_call(
        functools.partial(final_kernel, direct, shards),
        out_shape=[jax.ShapeDtypeStruct((ROWS, D), bf16), jax.ShapeDtypeStruct((ROWS, D), f32)]
        + [jax.ShapeDtypeStruct(g.shape, g.dtype) for g in grads] + [jax.ShapeDtypeStruct((n,), f32) for n in parts],
        in_specs=[SMEM] + [ANY] * 4 + [VMEM] * (1 + len(grads)),
        out_specs=[ANY] * 2 + [VMEM] * (len(grads) + len(parts)),
        scratch_shapes=[
            pltpu.VMEM((ROWS, D), bf16), pltpu.VMEM((SWAP, D), bf16), pltpu.VMEM((ROWS, D), bf16),
            pltpu.VMEM((SWAP, D), bf16), pltpu.VMEM((ROWS, D), f32),
            pltpu.SemaphoreType.DMA((tiles, 4)), pltpu.SemaphoreType.DMA((tiles, 2)),
        ],
        compiler_params=pltpu.CompilerParams(vmem_limit_bytes=VMEM_LIMIT),
        cost_estimate=pl.CostEstimate(flops=10**6, bytes_accessed=12 * 10**6, transcendentals=0),
        name="final",
    )(lens, out_own, out_in, ig_own, ig_in, vec, *grads)


def on_device(nz, direct, tokens, lens, gain1, shift1, wq, qb, vb, wp, pb, gain2, shift2, we, eb, ws, sb, cot):
    out_own, out_in, ig_own, ig_in, vec, _mid, *grads = layer_call(
        nz, direct, lens, tokens, cot, gain1, shift1, wq, qb, vb, wp, pb, gain2, shift2, we, eb, ws, sb)
    shards = lax.axis_size("batch") * 2
    out, ig, *rest = final_call(direct, shards, lens, out_own, out_in, ig_own, ig_in, vec, *(grads if direct else ()))
    if direct:
        gq, gp, ge, gs = rest[:4]
        parts = rest[4:]
    else:
        def scatter(g):
            return lax.psum_scatter(g, ("batch", "seq"), scatter_dimension=0, tiled=True)

        parts = [scatter(vec[i]) for i in range(8)] + [scatter(vec[8:12].reshape(FF))]
        us, ue = (g.astype(f32) for g in grads)
        gs = scatter(us.transpose(2, 1, 0, 3, 4).reshape(FF, D))
        ue = ue.reshape(8, 2, 4, 4, 2, 24, 384)
        wide = ue[:5].transpose(3, 2, 1, 5, 0, 4, 6).reshape(D, 5 * D)
        ge = scatter(wide[:, :FF])
        gp = scatter(wide[:, FF:])
        gq = ue[5:].reshape(3, 2, 4, 4, 2, 24, 3, 128).transpose(3, 2, 1, 5, 6, 0, 4, 7).reshape(D, 3 * D)
        gq = scatter(gq)
    return (out, ig, parts[0], parts[1], gq, parts[2], parts[3], gp, parts[4],
            parts[5], parts[6], ge, parts[8], gs, parts[7])


def solution(mesh):
    nz = mesh.shape["batch"] // 4
    direct = mesh.shape["batch"] == 16 and mesh.shape["seq"] == 2
    rows = P(("batch", "seq"), None)
    part = P(("batch", "seq"))
    whole = P()
    in_specs = (rows, P("batch", None)) + (whole,) * 13 + (rows,)
    out_specs = (rows, rows, part, part, rows, part, part, rows, part, part, part, rows, part, rows, part)
    return jax.shard_map(
        functools.partial(on_device, nz, direct),
        mesh=mesh, in_specs=in_specs, out_specs=out_specs, check_vma=False)
```

```python
import functools
import math

import jax
import jax.numpy as jnp
from jax import lax
from jax.experimental import pallas as pl
from jax.experimental.pallas import tpu as pltpu
from jax.sharding import PartitionSpec as P

f32 = jnp.float32
bf16 = jnp.bfloat16
MESH = pl.DeviceIdType.MESH
ANY = pl.BlockSpec(memory_space=pl.ANY)
VMEM = pl.BlockSpec(memory_space=pltpu.VMEM)
SMEM = pl.BlockSpec(memory_space=pltpu.SMEM)

H = 12
epsilon = 1e-05
masked_score = -1e30
ROWS = 1024
SWAP = 768
D = 768
FF = 3072
PAIRS = 6
BLK = 256
VMEM_LIMIT = 65000 * 2**10
GELU_C = 0.7978845608028654


def nn(a, b):
    return lax.dot_general(a, b, (((1,), (0,)), ((), ())), preferred_element_type=f32)


def nt(a, b):
    return lax.dot_general(a, b, (((1,), (1,)), ((), ())), preferred_element_type=f32)


def tn(a, b):
    return lax.dot_general(a, b, (((0,), (0,)), ((), ())), preferred_element_type=f32)


def row_stats(v):
    mean = jnp.mean(v, axis=-1, keepdims=True)
    centered = v - mean
    var = jnp.mean(centered * centered, axis=-1, keepdims=True)
    return centered * lax.rsqrt(var + epsilon), lax.rsqrt(var + epsilon)


def lane_ids(shape):
    return lax.broadcasted_iota(jnp.int32, shape, 1)


def row_ids(shape):
    return lax.broadcasted_iota(jnp.int32, shape, 0)


def split3(v):
    hi = v.astype(bf16).astype(f32)
    rest = v - hi
    mid = rest.astype(bf16).astype(f32)
    return hi, mid, rest - mid


def rotated(m, shift, i):
    coarse = lax.shift_right_logical(shift, 8)
    fine = lax.bitwise_and(shift, 255)

    def two(k):
        blocks = [m[pl.ds(pl.multiple_of(((i + k + n) % 4) * BLK, BLK), BLK), :] for n in range(2)]
        return jnp.concatenate(blocks, axis=0)

    part = jnp.where(coarse == 1, two(1), jnp.where(coarse == 2, two(2), two(3)))
    shape = (BLK, 2 * BLK)
    pick = (lane_ids(shape) == row_ids(shape) + fine).astype(f32).astype(bf16)
    return nn(pick, part)


def norm_back(v, gain, r):
    n, scale = row_stats(v)
    u = gain * r
    back = scale * (u - jnp.mean(u, axis=-1, keepdims=True) - n * jnp.mean(u * n, axis=-1, keepdims=True))
    return back, jnp.sum(r * n, axis=0, keepdims=True), jnp.sum(r, axis=0, keepdims=True)


def gelu_parts(e):
    sq = e * e
    th = jnp.tanh(e * (GELU_C + (GELU_C * 0.044715) * sq))
    half = 0.5 + 0.5 * th
    slope = half + (e * (1.0 - th * th)) * (0.5 * GELU_C + (1.5 * GELU_C * 0.044715) * sq)
    return e * half, slope


def spare_rows(*rows):
    ids = row_ids((64, rows[0].shape[1]))
    out = jnp.zeros(ids.shape, f32)
    for i, row in enumerate(rows):
        out = jnp.where(ids == i, row, out)
    return out


def with_spare(s, part, spare):
    return jnp.concatenate([part, spare] if s == 0 else [spare, part], axis=0).astype(bf16)


def layer_kernel(
    nz, direct,
    lens, tok_h, cot_h, gain1, shift1, wq_h, qb, vb, wp_h, pb, gain2, shift2, we_h, eb, ws_h, sb,
    *rest,
):
    n_out = 10 if direct else 8
    out_h, out_in_h, ig_h, ig_in_h, vec_h, mid_h = rest[:6]
    grads_h = rest[6:n_out]
    (gs, ge, tok_in, cot_in, m, cot, x, n1, q, qxt, kx, v, ctxt, acc, dn, n2, wq, wp, lse, vec, vec_in,
     load_sem, out_sem, swap_send, swap_recv) = rest[n_out : n_out + 25]
    if direct:
        (r0s, r0e, r1s, r1e, r2s, r2e, r3s, r3e, oq, op, oe, os_,
         s_send, s_recv, e_send, e_recv, j_send, j_recv, v_send, v_recv) = rest[n_out + 25 :]
    b = lax.axis_index("batch")
    c = lax.axis_index("seq")
    a = lens[0, 0]
    xx = b % 2
    yy = (b // 2) % 2
    zz = b // 4
    partner = (b, 1 - c)
    n1st = (b + (1 - c) * (1 - 2 * xx) + c * (2 - 4 * yy), c)
    n2nd = (b + c * (1 - 2 * xx) + (1 - c) * (2 - 4 * yy), c)
    zpeers = [(zz + i) % nz for i in range(1, nz)] if direct else []
    keep = [(1 - c) * (2 * k + xx) + c * (2 * yy + k) for k in range(2)]
    give = [(1 - c) * (2 * k + 1 - xx) + c * (2 * (1 - yy) + k) for k in range(2)]
    give2 = (1 - c) * (2 * (1 - yy) + xx) + c * (2 * yy + 1 - xx)
    home = 2 * yy + xx
    friends = [partner]
    if direct:
        cube = [(b - b % 4 + (yy + n // 2) % 2 * 2 + (xx + n) % 2, (c + n // 4) % 2) for n in range(1, 8)]
        friends = cube + [(b % 4 + 4 * z, c) for z in zpeers]

    def load(src, dst, i):
        return pltpu.make_async_copy(src, dst, load_sem.at[i])

    def remote(src, dst, send, recv, to):
        return pltpu.make_async_remote_copy(
            src_ref=src, dst_ref=dst, send_sem=send, recv_sem=recv,
            device_id=to, device_id_type=MESH)

    def place(u):
        return u if not direct else u % 5

    def column(u, to, slot):
        return remote(gs.at[c, home, u], r3s.at[slot], j_send.at[u], j_recv.at[slot], (b % 4 + 4 * to, c))

    def column_send(u):
        near = 2 - u // 2
        pl.when(zz == u + 1 - 2 * (u % 2))(lambda: column(u, u, 0).start())
        pl.when(zz == 3 - 3 * (u // 2))(lambda: column(u, near, 2 + u % 2).start())

    def column_pass(u):
        @pl.when(zz == 2 - u // 2)
        def _():
            column(u, u, 2 + u % 2).wait_recv()
            add_into(gs.at[c, home, u], r3s.at[2 + u % 2])
            column(u, u, 1).start()

    def copies(kind, u, stage):
        slot = u % 2
        if kind == "s":
            if stage == 0:
                return [remote(gs.at[1 - c, :, u], r0s.at[slot], s_send.at[u, 0], s_recv.at[u, 0], partner)]
            if stage == 1:
                return [remote(gs.at[c, give[k], u], r1s.at[u % 4, k], s_send.at[u, 1 + k], s_recv.at[u, 1 + k], n1st)
                        for k in range(2)]
            if stage == 2:
                return [remote(gs.at[c, give2, u], r2s.at[u % 4], s_send.at[u, 3], s_recv.at[u, 3], n2nd)]
            return [column(u, u, 0)]
        g = ge.at[place(u)]
        if stage == 0:
            return [remote(g.at[1 - c], r0e.at[slot], e_send.at[u, 0], e_recv.at[u, 0], partner)]
        if stage == 1:
            return [remote(g.at[c, give[k]], r1e.at[u % 4, k], e_send.at[u, 1 + k], e_recv.at[u, 1 + k], n1st)
                    for k in range(2)]
        if stage == 2:
            return [remote(g.at[c, give2], r2e.at[u % 4], e_send.at[u, 3], e_recv.at[u, 3], n2nd)]
        return [remote(g.at[c, home, z], r3e.at[u % 4, i], e_send.at[u, 4 + i], e_recv.at[u, 4 + i],
                       (b % 4 + 4 * z, c)) for i, z in enumerate(zpeers)]

    def start(kind, u, stage):
        if direct:
            for cp in copies(kind, u, stage):
                cp.start()

    def finish(kind, u, stage):
        for cp in copies(kind, u, stage):
            cp.wait()

    def add_into(dst, src):
        dst[...] = dst[...] + src[...]

    def advance(kind, u, stage):
        finish(kind, u, stage - 1)
        slot = u % 2
        if kind == "s":
            if stage == 1:
                for k in range(4):
                    add_into(gs.at[c, k, u], r0s.at[slot, k])
            elif stage == 2:
                for k in range(2):
                    add_into(gs.at[c, keep[k], u], r1s.at[u % 4, k])
            elif stage == 3:
                add_into(gs.at[c, home, u], r2s.at[u % 4])
        else:
            g = ge.at[place(u), c]
            if stage == 1:
                for k in range(4):
                    add_into(g.at[k], r0e.at[slot, k])
            elif stage == 2:
                for k in range(2):
                    add_into(g.at[keep[k]], r1e.at[u % 4, k])
            elif stage == 3:
                add_into(g.at[home], r2e.at[u % 4])
        if kind == "s" and stage == 3:
            column_send(u)
        else:
            start(kind, u, stage)

    def settle(kind, u):
        if kind == "s":
            for n in range(nz):
                pl.when(zz != n)(lambda n=n: copies("s", n, 3)[0].wait_send())
            for i in range(2):
                column(0, 0, i).wait_recv()
            total = gs[c, home, zz].astype(f32)
            for i in range(2):
                total = total + r3s[i].astype(f32)
            os_[...] = total
            return
        finish(kind, u, 3)
        total = ge[place(u), c, home, zz].astype(f32)
        for i in range(nz - 1):
            total = total + r3e[u % 4, i].astype(f32)
        for h in range(2):
            half = total[24 * h : 24 * h + 24, :]
            if u < 4:
                oe[:, 768 * u + 384 * h : 768 * u + 384 * h + 384] = half
            elif u == 4:
                op[:, 384 * h : 384 * h + 384] = half
            else:
                for w in range(3):
                    at = 768 * w + 256 * (u - 5) + 128 * h
                    oq[:, at : at + 128] = half[:, 128 * w : 128 * w + 128]

    def steps(todo, when=None):
        if not direct:
            return

        def act():
            for kind, u, stage in todo:
                if stage == 4:
                    settle(kind, u)
                elif stage == "pass":
                    column_pass(u)
                else:
                    advance(kind, u, stage)

        if when is None:
            act()
        else:
            pl.when(when)(act)

    lane = lane_ids((BLK, 128))
    tiles = ROWS // BLK
    chunk = FF // 4

    def merge(own, other):
        def step(i, _):
            rows = pl.ds(pl.multiple_of(i * BLK, BLK), BLK)
            mine = row_ids((BLK, D)) + i * BLK >= a
            own[rows, :] = jnp.where(mine, own[rows, :].astype(f32), other[rows, :].astype(f32)).astype(bf16)
            return 0
        lax.fori_loop(0, SWAP // BLK, step, 0)

    def turn(src, dst, shift):
        def step(i, _):
            dst[pl.ds(pl.multiple_of(i * BLK, BLK), BLK), :] = rotated(src, shift, i).astype(bf16)
            return 0
        lax.fori_loop(0, tiles, step, 0)

    def expand_shares(slot, i, g):
        half = g.shape[1] // 2
        for n in range(16):
            part = g[24 * n : 24 * n + 24, :]
            part = jnp.concatenate([part[:, 0:half], part[:, half:]], axis=0).astype(bf16)
            yield (slot, n % 2, (n // 2) % 4, 2 * i + n // 8), part

    def front(we, ws, vt):
        loads = [load(src, dst, i) for i, (src, dst) in enumerate(
            ((tok_h, m), (wq_h, wq), (cot_h, n2), (wp_h, wp), (we_h, we), (ws_h, ws)))]
        for cp in loads[:4]:
            cp.start()
        swaps = [
            remote(src.at[pl.ds(0, SWAP)], dst, swap_send.at[i], swap_recv.at[i], partner)
            for i, (src, dst) in enumerate(((tok_h, tok_in), (cot_h, cot_in)))
        ]
        barrier = pltpu.get_barrier_semaphore()
        for f in friends:
            pl.semaphore_signal(barrier, inc=1, device_id=f, device_id_type=MESH)
        pl.semaphore_wait(barrier, len(friends))
        for cp in swaps:
            cp.start()
        for cp in loads[4:]:
            cp.start()
        vec[...] = jnp.zeros_like(vec)
        dn[...] = jnp.zeros_like(dn)
        loads[0].wait()
        swaps[0].wait()
        merge(m, tok_in)
        loads[1].wait()
        bound = jnp.where(c == 0, 0, ROWS - a)

        def project(i, _):
            r = pl.multiple_of(i * BLK, BLK)
            rows = pl.ds(r, BLK)
            xt = rotated(m, a, i)
            x[rows, :] = xt.astype(bf16)
            normed, _unused = row_stats(xt)
            nt_ = (normed * gain1[...].reshape(1, D) + shift1[...].reshape(1, D)).astype(bf16)
            n1[rows, :] = nt_
            qt = nn(nt_, wq[:, 0:D]) + qb[...].reshape(1, D)
            qt = (qt.astype(bf16).astype(f32) * 0.125).astype(bf16)
            q[rows, :] = qt
            qtt = qt.T
            k = nn(nt_, wq[:, D : 2 * D])
            vv = (nn(nt_, wq[:, 2 * D : 3 * D]) + vb[...].reshape(1, D)).astype(bf16)
            v[rows, :] = vv
            vt[:, rows] = vv.T
            k_flag = jnp.where(row_ids((BLK, 128)) + r >= bound, 0.0, masked_score).astype(f32)
            q_flag = jnp.where(lane_ids((1, BLK)) + r >= bound, 1.0, 0.0).astype(f32)
            q_spare = spare_rows(q_flag)
            for p in range(PAIRS):
                kp = k[:, 128 * p : 128 * p + 128]
                for s in range(2):
                    mine = lane < 64 if s == 0 else lane >= 64
                    base = 64 if s == 0 else 0
                    k_aug = jnp.where(lane == base, k_flag, 1.0)
                    k_aug = jnp.where(lane > base + 3, 0.0, k_aug)
                    at = 256 * p + 128 * s
                    kx[rows, at : at + 128] = jnp.where(mine, kp, k_aug).astype(bf16)
                    qxt[at : at + 128, rows] = with_spare(
                        s, qtt[128 * p + 64 * s : 128 * p + 64 * s + 64, :].astype(f32), q_spare)
            return 0

        lax.fori_loop(0, tiles, project, 0)
        triangle = row_ids((BLK, BLK)) <= lane_ids((BLK, BLK))
        jobs = [(i, s) for i in range(tiles) for s in range(2)]

        def attend(p, _):
            at = pl.multiple_of(p * 256, 256)
            pat = pl.multiple_of(p * 128, 128)

            def scores(i, s):
                qt = qxt[pl.ds(at + 128 * s, 128), BLK * i : BLK * i + BLK]
                st = [nn(kx[BLK * k : BLK * k + BLK, pl.ds(at + 128 * s, 128)], qt) for k in range(i + 1)]
                st[i] = jnp.where(triangle, st[i], masked_score)
                return st

            ready = [scores(*job) for job in jobs[:2]]
            for n, (i, s) in enumerate(jobs):
                st = ready.pop(0)
                if n + 2 < len(jobs):
                    ready.append(scores(*jobs[n + 2]))
                cols = slice(BLK * i, BLK * i + BLK)
                peak = jnp.max(st[0], axis=0, keepdims=True)
                for t in st[1:]:
                    peak = jnp.maximum(peak, jnp.max(t, axis=0, keepdims=True))
                vv = jnp.concatenate([vt[pl.ds(pat + 64 * s, 64), :], jnp.ones((16, ROWS), bf16)], axis=0)
                weights = [jnp.exp(t - peak).astype(bf16) for t in st]
                weights = weights[0] if i == 0 else jnp.concatenate(weights, axis=0)
                o = nn(vv[:, 0 : BLK * (i + 1)], weights)
                total = o[64:65, :]
                ctxt[pl.ds(pat + 64 * s, 64), cols] = (o[0:64, :] / total).astype(bf16)
                lse[pl.ds(2 * p + s, 1), cols] = peak + jnp.log(total)
            return 0

        lax.fori_loop(0, PAIRS, attend, 0)
        every = jnp.where(lane_ids((1, ROWS)) >= bound, 1.0, 0.0).astype(f32)
        for h in range(H):
            spare = spare_rows(every, *split3(-lse[h : h + 1, :]))
            at = 128 * h + (64 if h % 2 == 0 else 0)
            qxt[at : at + 64, :] = spare.astype(bf16)
        loads[2].wait()
        swaps[1].wait()
        merge(n2, cot_in)
        turn(n2, cot, a)
        loads[3].wait()

        def add_attended(i, _):
            rows = pl.ds(pl.multiple_of(i * BLK, BLK), BLK)
            mid = tn(ctxt[:, rows], wp[...]) + pb[...].reshape(1, D) + x[rows, :].astype(f32)
            acc[rows, :] = mid
            normed, _unused = row_stats(mid)
            n2[rows, :] = (normed * gain2[...].reshape(1, D) + shift2[...].reshape(1, D)).astype(bf16)
            pltpu.make_async_copy(acc.at[rows], mid_h.at[rows], load_sem.at[6]).start()
            return 0

        lax.fori_loop(0, tiles, add_attended, 0)
        load(acc, mid_h, 6).wait()
        loads[4].wait()
        loads[5].wait()

    def feed_forward(we, ws, grad):
        low = m

        def one(j, _):
            cols = pl.ds(pl.multiple_of(j * chunk, chunk), chunk)

            def products(t):
                rows = slice(t * BLK, t * BLK + BLK)
                return (nn(n2[rows, :], we[:, cols]) + eb[cols].reshape(1, chunk),
                        nt(cot[rows, :], ws[cols, :]))

            bias_sum = jnp.zeros((1, chunk), f32)
            ready = products(0)
            for t in range(tiles):
                e, da = ready
                if t + 1 < tiles:
                    ready = products(t + 1)
                rows = slice(t * BLK, t * BLK + BLK)
                act, slope = gelu_parts(e)
                act = act.astype(bf16)
                de = (da * slope).astype(bf16)
                low[rows, :] = act
                grad[rows, :] = de
                acc[rows, :] += nn(act, ws[cols, :])
                dn[rows, :] += nt(de, we[:, cols])
                bias_sum = bias_sum + jnp.sum(de.astype(f32), axis=0, keepdims=True)
                if t == 0:
                    steps([("s", j - 3, 3)], j >= 3)
                    steps([("s", j - 2, 2)], j >= 2)
                elif t == 1:
                    steps([("s", j - 1, 1)], j >= 1)
                elif t == 2:
                    steps([("e", j - 3, 2)], j >= 3)
                else:
                    steps([("e", j - 1, 1)], j >= 1)
            vec[pl.ds(8 + j, 1), :] = bias_sum
            for i in range(2):
                g = tn(low[:, 384 * i : 384 * i + 384], cot[...]).astype(bf16)
                for n in range(4):
                    gs[n % 2, 2 * i + n // 2, j] = g[96 * n : 96 * n + 96, :]
            start("s", j, 0)
            for i in range(2):
                for at, part in expand_shares(j, i, tn(n2[:, 384 * i : 384 * i + 384], grad[...])):
                    ge[at] = part
            start("e", j, 0)
            return 0

        lax.fori_loop(0, 4, one, 0)

    def first_half(we, ws):
        pl.run_scoped(functools.partial(front, we, ws), pltpu.VMEM((D, ROWS), bf16))
        pl.run_scoped(functools.partial(feed_forward, we, ws), pltpu.VMEM((ROWS, chunk), bf16))

    pl.run_scoped(first_half, pltpu.VMEM((D, FF), bf16), pltpu.VMEM((FF, D), bf16))
    def total_copies(n):
        to = cube if n == 0 else [(b % 4 + 4 * z, c) for z in zpeers]
        at = 7 * n
        return [remote(vec, vec_in.at[at + i], v_send.at[at + i], v_recv.at[at + i], t) for i, t in enumerate(to)]

    def total_hop(n):
        for cp in total_copies(n):
            cp.wait()
        total = vec[...]
        for i in range(len(total_copies(n))):
            total = total + vec_in[7 * n + i]
        vec[...] = total

    out_give = [remote(cot.at[pl.ds(0, SWAP)], out_in_h, swap_send.at[2], swap_recv.at[2], partner),
                pltpu.make_async_copy(cot, out_h, out_sem.at[0])]
    ig_give = [remote(n2.at[pl.ds(0, SWAP)], ig_in_h, swap_send.at[3], swap_recv.at[3], partner),
               pltpu.make_async_copy(n2, ig_h, out_sem.at[1])]

    def middle(dot, do):
        def second(mid, ga_all):
            own = load(mid_h, mid, 6)
            own.start()
            own.wait()

            def tile(i, sums):
                rows = slice(i * BLK, i * BLK + BLK)
                m[rows, :] = (acc[rows, :] + sb[...].reshape(1, D)).astype(bf16)
                back, dgain, dshift = norm_back(mid[rows, :], gain2[...].reshape(1, D), dn[rows, :])
                ct = cot[rows, :].astype(f32)
                dmid = ct + back
                dn[rows, :] = dmid
                ga = dmid.astype(bf16)
                ga_all[rows, :] = ga
                dc = nt(ga, wp[...]).astype(bf16)
                do[rows, :] = dc
                dct = dc.T.astype(f32)
                prod = dct * ctxt[:, rows].astype(f32)
                for h in range(H):
                    inner = jnp.sum(prod[64 * h : 64 * h + 64, :], axis=0, keepdims=True)
                    dot[128 * h : 128 * h + 128, rows] = with_spare(
                        h % 2, dct[64 * h : 64 * h + 64, :], spare_rows(*split3(-inner)))
                for n, todo in enumerate((
                    [("s", 2, 2), ("s", 3, 1), ("s", 0, "pass")], [("s", 1, 3), ("e", 3, 1)], [("e", 1, 2)], [("e", 0, 3)])):
                    if i == n:
                        steps(todo)
                dpb = jnp.sum(ga.astype(f32), axis=0, keepdims=True)
                dsb = jnp.sum(ct, axis=0, keepdims=True)
                return tuple(o + n for o, n in zip(sums, (dgain, dshift, dpb, dsb)))

            zero = jnp.zeros((1, D), f32)
            sums = (zero,) * 4
            for i in range(tiles):
                sums = tile(i, sums)
            for at, s in zip((5, 6, 4, 7), sums):
                vec[at : at + 1, :] = s
            turn(m, cot, ROWS - a)
            for cp in out_give:
                cp.start()
            for i in range(2):
                for at, part in expand_shares(place(4), i, nn(ctxt[384 * i : 384 * i + 384, :], ga_all[...])):
                    ge[at] = part
            start("e", 4, 0)

        pl.run_scoped(second, pltpu.VMEM((ROWS, D), f32), pltpu.VMEM((ROWS, D), bf16))

    def attention(dot, do, dqkv):
        triangle = row_ids((BLK, BLK)) <= lane_ids((BLK, BLK))
        jobs = [(kb, qi, s) for kb in range(tiles) for qi in range(kb, tiles) for s in range(2)]

        def attention_loop(ktr, dqt):
            def pair(p, _):
                at = pl.multiple_of(p * 256, 256)
                pat = pl.multiple_of(p * 128, 128)
                pcols = pl.ds(pat, 128)
                lf = lane_ids((ROWS, 128))
                ktr[...] = jnp.where(lf < 64, kx[:, pl.ds(at, 128)], kx[:, pl.ds(at + 128, 128)]).T

                def scores(kb, qi, s):
                    krows = slice(BLK * kb, BLK * kb + BLK)
                    qrows = slice(BLK * qi, BLK * qi + BLK)
                    head = pl.ds(at + 128 * s, 128)
                    vd = v[krows, pcols]
                    vd = jnp.where(lane < 64 if s == 0 else lane >= 64, vd, jnp.ones_like(vd))
                    return nn(kx[krows, head], qxt[head, qrows]), nn(vd, dot[head, qrows])

                ready = [scores(*job) for job in jobs[:2]]
                dk, dv = {}, {}
                dv_sum = jnp.zeros((1, 128), f32)
                for n, (kb, qi, s) in enumerate(jobs):
                    st, dp = ready.pop(0)
                    if n + 2 < len(jobs):
                        ready.append(scores(*jobs[n + 2]))
                    krows = slice(BLK * kb, BLK * kb + BLK)
                    qrows = slice(BLK * qi, BLK * qi + BLK)
                    prob = jnp.exp(st)
                    if qi == kb:
                        prob = jnp.where(triangle, prob, 0.0)
                    ds = (prob * dp).astype(bf16)
                    dv_part = nn(prob.astype(bf16), do[qrows, pcols])
                    dk_part = nn(ds, q[qrows, pcols])
                    dv[s] = dv_part if qi == kb else dv[s] + dv_part
                    dk[s] = dk_part if qi == kb else dk[s] + dk_part
                    half = slice(64 * s, 64 * s + 64)
                    dq_part = nn(ktr[half, krows], ds)
                    if kb == 0:
                        dqt[half, qrows] = dq_part
                    else:
                        dqt[half, qrows] += dq_part
                    if s == 1 and qi == tiles - 1:
                        dqkv[krows, pl.ds(D + pat, 128)] = jnp.where(lane < 64, dk[0], dk[1]).astype(bf16)
                        dvp = jnp.where(lane < 64, dv[0], dv[1]).astype(bf16)
                        dqkv[krows, pl.ds(2 * D + pat, 128)] = dvp
                        dv_sum = dv_sum + jnp.sum(dvp.astype(f32), axis=0, keepdims=True)
                dq = (dqt[...] * 0.125).astype(bf16).T
                dqkv[:, pcols] = dq
                vec[2:3, pcols] = jnp.sum(dq.astype(f32), axis=0, keepdims=True)
                vec[3:4, pcols] = dv_sum
                for r, todo in enumerate((
                    [("s", 3, 2), ("s", 2, 3), ("e", 2, 2), ("e", 4, 1), ("s", 1, "pass")],
                    [("e", 0, 4), ("s", 3, 3), ("e", 1, 3), ("e", 3, 2), ("s", 2, "pass")],
                    [("e", 2, 3), ("e", 4, 2), ("e", 5, 1), ("s", 3, "pass")],
                    [("e", 1, 4), ("e", 3, 3)],
                    [("e", 2, 4), ("e", 4, 3), ("e", 5, 2), ("e", 6, 1)],
                    [("e", 3, 4)])):
                    steps(todo, p == r)
                @pl.when(p % 2 == 1)
                def _():
                    k = p // 2
                    for i in range(2):
                        for w in range(3):
                            cols = pl.ds(pl.multiple_of(768 * w + 256 * k, 256), 256)
                            g = tn(n1[:, 384 * i : 384 * i + 384], dqkv[:, cols])
                            for at_, part in expand_shares(place(5 + k), i, g):
                                ge[at_ + (slice(None), slice(128 * w, 128 * w + 128))] = part
                    start("e", 5 + k, 0)

                steps([("e", 6, 2)], p == PAIRS - 1)
                return 0

            lax.fori_loop(0, PAIRS, pair, 0)

        pl.run_scoped(attention_loop, pltpu.VMEM((128, ROWS), bf16), pltpu.VMEM((128, ROWS), f32))

        def tile(i, sums):
            rows = pl.ds(pl.multiple_of(i * BLK, BLK), BLK)
            g = nt(dqkv[rows, :], wq[...])
            back, dgain, dshift = norm_back(x[rows, :].astype(f32), gain1[...].reshape(1, D), g)
            m[rows, :] = (dn[rows, :] + back).astype(bf16)
            for n, todo in enumerate((
                [("e", 7, 1), ("e", 4, 4), ("e", 5, 3)], [("s", 0, 4)], [("e", 6, 3)], [("e", 7, 2)])):
                steps(todo, i == n)
            return sums[0] + dgain, sums[1] + dshift

        zero = jnp.zeros((1, D), f32)
        sums = lax.fori_loop(0, tiles, tile, (zero,) * 2)
        vec[0:1, :] = sums[0]
        vec[1:2, :] = sums[1]
        if direct:
            for cp in total_copies(0):
                cp.start()
        turn(m, n2, ROWS - a)
        for cp in ig_give:
            cp.start()

    def second_half(dot, do):
        middle(dot, do)
        pl.run_scoped(functools.partial(attention, dot, do), pltpu.VMEM((ROWS, 3 * D), bf16))

    pl.run_scoped(second_half, pltpu.VMEM((2 * D, ROWS), bf16), pltpu.VMEM((ROWS, D), bf16))

    ends = list(out_give + ig_give)

    def emit(src, dst):
        cp = pltpu.make_async_copy(src, dst, out_sem.at[len(ends) - 2])
        cp.start()
        ends.append(cp)

    if direct:
        steps([("e", 5, 4), ("e", 7, 3)])
        total_hop(0)
        for cp in total_copies(1):
            cp.start()
        steps([("e", 6, 4), ("e", 7, 4)])
        total_hop(1)
        emit(vec, vec_h)
        for src, dst in zip((oq, op, oe, os_), grads_h):
            emit(src, dst)
    else:
        emit(vec, vec_h)
        emit(gs, grads_h[0])
        emit(ge, grads_h[1])
    for cp in ends:
        cp.wait()


def layer_call(nz, direct, *args):
    unit = (48, 384)
    if direct:
        grads = [((24, 3 * D), f32), ((24, D), f32), ((24, FF), f32), ((96, D), f32)]
    else:
        grads = [((2, 4, 4, 96, D), bf16), ((8, 2, 4, 4) + unit, bf16)]
    shapes = [((ROWS, D), bf16), ((SWAP, D), bf16), ((ROWS, D), bf16), ((SWAP, D), bf16), ((16, D), f32),
              ((ROWS, D), f32)] + grads
    scratch = [
        pltpu.VMEM((2, 4, 4, 96, D), bf16), pltpu.VMEM((5 if direct else 8, 2, 4, 4) + unit, bf16),
        pltpu.VMEM((SWAP, D), bf16), pltpu.VMEM((SWAP, D), bf16),
        pltpu.VMEM((ROWS, D), bf16), pltpu.VMEM((ROWS, D), bf16),
        pltpu.VMEM((ROWS, D), bf16), pltpu.VMEM((ROWS, D), bf16),
        pltpu.VMEM((ROWS, D), bf16),
        pltpu.VMEM((2 * D, ROWS), bf16), pltpu.VMEM((ROWS, 2 * D), bf16),
        pltpu.VMEM((ROWS, D), bf16), pltpu.VMEM((D, ROWS), bf16),
        pltpu.VMEM((ROWS, D), f32), pltpu.VMEM((ROWS, D), f32),
        pltpu.VMEM((ROWS, D), bf16),
        pltpu.VMEM((D, 3 * D), bf16), pltpu.VMEM((D, D), bf16),
        pltpu.VMEM((16, ROWS), f32),
        pltpu.VMEM((16, D), f32), pltpu.VMEM((10 if direct else 1, 16, D), f32),
        pltpu.SemaphoreType.DMA((7,)), pltpu.SemaphoreType.DMA((8,)),
        pltpu.SemaphoreType.DMA((4,)), pltpu.SemaphoreType.DMA((4,)),
    ]
    if direct:
        scratch += [
            pltpu.VMEM((2, 4, 96, D), bf16), pltpu.VMEM((2, 4, nz) + unit, bf16),
            pltpu.VMEM((4, 2, 96, D), bf16), pltpu.VMEM((4, 2, nz) + unit, bf16),
            pltpu.VMEM((4, 96, D), bf16), pltpu.VMEM((4, nz) + unit, bf16),
            pltpu.VMEM((4, 96, D), bf16), pltpu.VMEM((4, nz - 1) + unit, bf16),
            pltpu.VMEM((24, 3 * D), f32), pltpu.VMEM((24, D), f32), pltpu.VMEM((24, FF), f32), pltpu.VMEM((96, D), f32),
            pltpu.SemaphoreType.DMA((4, 4)), pltpu.SemaphoreType.DMA((4, 4)),
            pltpu.SemaphoreType.DMA((8, 7)), pltpu.SemaphoreType.DMA((8, 7)),
            pltpu.SemaphoreType.DMA((nz,)), pltpu.SemaphoreType.DMA((4,)),
            pltpu.SemaphoreType.DMA((10,)), pltpu.SemaphoreType.DMA((10,)),
        ]
    return pl.pallas_call(
        functools.partial(layer_kernel, nz, direct),
        out_shape=[jax.ShapeDtypeStruct(s, t) for s, t in shapes],
        in_specs=[SMEM, ANY, ANY, VMEM, VMEM, ANY, VMEM, VMEM, ANY, VMEM, VMEM, VMEM, ANY, VMEM, ANY, VMEM],
        out_specs=[ANY] * len(shapes),
        scratch_shapes=scratch,
        compiler_params=pltpu.CompilerParams(
            collective_id=0, has_side_effects=True, vmem_limit_bytes=VMEM_LIMIT),
        cost_estimate=pl.CostEstimate(
            flops=64 * 10**9, bytes_accessed=40 * 10**6, transcendentals=20 * 10**6),
        name="layer",
    )(*args)


def final_kernel(
    direct, shards, lens, out_own, out_in, ig_own, ig_in, vec, *rest,
):
    moved = 4 if direct else 0
    given = 9 if direct else 0
    grads = rest[:moved]
    out, ig = rest[moved : moved + 2]
    grads_to = rest[moved + 2 : 2 * moved + 2]
    parts = rest[2 * moved + 2 : 2 * moved + 2 + given]
    own, inn, igo, igi, res, load_sem, save_sem = rest[2 * moved + 2 + given :]
    a = lens[0, 0]
    tiles = ROWS // BLK
    loads = []
    for t in range(tiles):
        rows = pl.ds(t * BLK, BLK)
        some = [(ig_own, igo), (out_own, own)]
        if t * BLK < SWAP:
            some += [(ig_in, igi), (out_in, inn)]
        loads.append([pltpu.make_async_copy(src.at[rows], dst.at[rows], load_sem.at[t, i])
                      for i, (src, dst) in enumerate(some)])
    for group in loads:
        for cp in group:
            cp.start()
    saves = []
    for t in range(tiles):
        for cp in loads[t]:
            cp.wait()
        rows = slice(t * BLK, t * BLK + BLK)
        g = igo[rows, :].astype(f32)
        if t * BLK < SWAP:
            mine = row_ids((BLK, D)) + t * BLK >= a
            own[rows, :] = jnp.where(mine, own[rows, :].astype(f32), inn[rows, :].astype(f32)).astype(bf16)
            g = jnp.where(mine, g, igi[rows, :].astype(f32))
        res[rows, :] = g
        for i, (src, dst) in enumerate(((own, out), (res, ig))):
            saves.append(pltpu.make_async_copy(src.at[pl.ds(t * BLK, BLK)], dst.at[pl.ds(t * BLK, BLK)], save_sem.at[t, i]))
            saves[-1].start()
    for src, dst in zip(grads, grads_to):
        dst[...] = src[...]
    if direct:
        me = lax.axis_index("batch") * 2 + lax.axis_index("seq")

        def columns(v, first, n):
            shape = (D, 128)
            pick = (row_ids(shape) == lane_ids(shape) + first) & (lane_ids(shape) < n)
            return jnp.dot(v, pick.astype(f32), precision=lax.Precision.HIGHEST, preferred_element_type=f32)

        n = D // shards
        narrow = columns(vec[...], n * me, n)
        for i in range(8):
            parts[i][...] = narrow[i, :n]
        n = FF // shards
        wide = columns(vec[8:12, :], n * (me % (D // n)), n)
        wide = jnp.sum(jnp.where(row_ids(wide.shape) == me // (D // n), wide, 0.0), axis=0)
        parts[8][...] = wide[:n]
    for cp in saves:
        cp.wait()


def final_call(direct, shards, lens, out_own, out_in, ig_own, ig_in, vec, *grads):
    tiles = ROWS // BLK
    parts = [D // shards] * 8 + [FF // shards] if direct else []
    return pl.pallas_call(
        functools.partial(final_kernel, direct, shards),
        out_shape=[jax.ShapeDtypeStruct((ROWS, D), bf16), jax.ShapeDtypeStruct((ROWS, D), f32)]
        + [jax.ShapeDtypeStruct(g.shape, g.dtype) for g in grads] + [jax.ShapeDtypeStruct((n,), f32) for n in parts],
        in_specs=[SMEM] + [ANY] * 4 + [VMEM] * (1 + len(grads)),
        out_specs=[ANY] * 2 + [VMEM] * (len(grads) + len(parts)),
        scratch_shapes=[
            pltpu.VMEM((ROWS, D), bf16), pltpu.VMEM((SWAP, D), bf16), pltpu.VMEM((ROWS, D), bf16),
            pltpu.VMEM((SWAP, D), bf16), pltpu.VMEM((ROWS, D), f32),
            pltpu.SemaphoreType.DMA((tiles, 4)), pltpu.SemaphoreType.DMA((tiles, 2)),
        ],
        compiler_params=pltpu.CompilerParams(vmem_limit_bytes=VMEM_LIMIT),
        cost_estimate=pl.CostEstimate(flops=10**6, bytes_accessed=12 * 10**6, transcendentals=0),
        name="final",
    )(lens, out_own, out_in, ig_own, ig_in, vec, *grads)


def on_device(nz, direct, tokens, lens, gain1, shift1, wq, qb, vb, wp, pb, gain2, shift2, we, eb, ws, sb, cot):
    out_own, out_in, ig_own, ig_in, vec, _mid, *grads = layer_call(
        nz, direct, lens, tokens, cot, gain1, shift1, wq, qb, vb, wp, pb, gain2, shift2, we, eb, ws, sb)
    shards = lax.axis_size("batch") * 2
    out, ig, *rest = final_call(direct, shards, lens, out_own, out_in, ig_own, ig_in, vec, *(grads if direct else ()))
    if direct:
        gq, gp, ge, gs = rest[:4]
        parts = rest[4:]
    else:
        def scatter(g):
            return lax.psum_scatter(g, ("batch", "seq"), scatter_dimension=0, tiled=True)

        parts = [scatter(vec[i]) for i in range(8)] + [scatter(vec[8:12].reshape(FF))]
        us, ue = (g.astype(f32) for g in grads)
        gs = scatter(us.transpose(2, 1, 0, 3, 4).reshape(FF, D))
        ue = ue.reshape(8, 2, 4, 4, 2, 24, 384)
        wide = ue[:5].transpose(3, 2, 1, 5, 0, 4, 6).reshape(D, 5 * D)
        ge = scatter(wide[:, :FF])
        gp = scatter(wide[:, FF:])
        gq = ue[5:].reshape(3, 2, 4, 4, 2, 24, 3, 128).transpose(3, 2, 1, 5, 6, 0, 4, 7).reshape(D, 3 * D)
        gq = scatter(gq)
    return (out, ig, parts[0], parts[1], gq, parts[2], parts[3], gp, parts[4],
            parts[5], parts[6], ge, parts[8], gs, parts[7])


def solution(mesh):
    nz = mesh.shape["batch"] // 4
    direct = mesh.shape["batch"] == 16 and mesh.shape["seq"] == 2
    rows = P(("batch", "seq"), None)
    part = P(("batch", "seq"))
    whole = P()
    in_specs = (rows, P("batch", None)) + (whole,) * 13 + (rows,)
    out_specs = (rows, rows, part, part, rows, part, part, rows, part, part, part, rows, part, rows, part)
    return jax.shard_map(
        functools.partial(on_device, nz, direct),
        mesh=mesh, in_specs=in_specs, out_specs=out_specs, check_vma=False)
```
